512 devices in a mesh: rep: 64 (over z_lo, x, core), gz: 8 (over z_hi, y).
Axes of the slice: x: 4, y: 4, z: 16 (z_hi: 2, z_lo: 8; z = z_hi * 8 + z_lo), core: 2. Of those that a mesh axis runs over, the one named last changes fastest.
Arguments:
- layer_input: bfloat16 [64, 16, 32, 16, 128], P('rep', 'gz'), may hold values from -6 to 6
- pre_act: bfloat16 [64, 16, 32, 16, 128], P('rep', 'gz'), may hold values from -6 to 6
- cotangent: bfloat16 [64, 16, 32, 16, 128], P('rep', 'gz'), may hold values from -6 to 6
- w_one: bfloat16 [27, 128, 128], replicated, may hold values from -0.109375 to 0.109375
- w_two: bfloat16 [27, 128, 128], replicated, may hold values from -0.109375 to 0.109375
Outputs:
- input_grad: bfloat16 [64, 16, 32, 16, 128], P('rep', 'gz')
- grad_one: float32 [3456, 128], P('rep', 'gz')
- grad_two: float32 [3456, 128], P('rep', 'gz')
The draws below stay inside these ranges and needn't reach their ends.
All inputs are finite; a program needn't handle non-finite values.
Results may differ from the reference program's by a relative error of at most 0.015.
Values may be sent and summed in bfloat16 or wider, within the bound.
A program may use at most 64 MiB of HBM per device.

```python
import math
import jax
import jax.numpy as jnp
from jax import lax

CH = 128
TAPS = 27
EDGE_Y = 32
EDGE_X = 16
SAMPLES = 64
NZ = 16
CELLS = 524288


def strengthened(result, stream_key, source, target, shards_of, factor):
    owner, partner = [(jnp.arange(result.shape[dim]) // (result.shape[dim] // shards_of)).reshape([-1 if axis == dim else 1 for axis in range(result.ndim)]) for dim in (source, target)]
    chosen = jax.random.permutation(stream_key, shards_of)[partner]
    strong = (owner == chosen) | (owner == (partner + shards_of // 2) % shards_of)
    return jnp.where(strong, factor * result, result)


def block_levels(key, extent, pieces, least, largest):
    gain, own = 1.0, jax.random.fold_in(key, 6)
    for position, shards_of in pieces:
        draws = jnp.exp(jax.random.uniform(jax.random.fold_in(own, position), (shards_of,), jnp.float32, least / len(pieces), largest / len(pieces)))
        gain = gain * jnp.repeat(draws, extent[position] // shards_of).reshape([-1 if axis == position else 1 for axis in range(len(extent))])
    return gain


def scatter_about(rng, shape, deviation, most, cuts=(), dtype=jnp.bfloat16):
    values = jax.random.normal(rng, shape, jnp.float32) * deviation
    if len(cuts) > 0:
        values = block_levels(rng, shape, cuts, -0.22, 0.18) * values
    return jnp.clip(values, min=-most, max=most).astype(dtype)


def bell_draw_with(own_key, extent, deviation, bound, cuts, heavy, held_as=jnp.bfloat16):
    drawn = deviation * jax.random.normal(own_key, extent, jnp.float32)
    if cuts:
        drawn = drawn * block_levels(own_key, extent, cuts, -0.22, 0.18)
    return jnp.clip(strengthened(drawn, jax.random.fold_in(own_key, 3), *heavy), -bound, bound).astype(held_as)


def setup_inputs(seed: int = 0) -> dict:
    key_of = jax.random.split(jax.random.key(seed), 6)
    layer_input = scatter_about(key_of[0], (SAMPLES, NZ, EDGE_Y, EDGE_X, CH), 1.0, 6.0, ((0, 64), (1, 8)))
    pre_act = scatter_about(key_of[1], (SAMPLES, NZ, EDGE_Y, EDGE_X, CH), 1.0, 6.0, ((0, 64), (1, 8)))
    cotangent = bell_draw_with(key_of[2], (SAMPLES, NZ, EDGE_Y, EDGE_X, CH), 1.0, 6.0, ((0, 64), (1, 8)), (1, 4, 8, 2.0))
    w_one = scatter_about(key_of[3], (TAPS, CH, CH), (TAPS * CH) ** -0.5, 0.109375)
    w_two = scatter_about(key_of[4], (TAPS, CH, CH), (TAPS * CH) ** -0.5, 0.109375)
    return {"layer_input": layer_input, "pre_act": pre_act, "cotangent": cotangent, "w_one": w_one, "w_two": w_two}


leak_slope = 0.3

def data_grad(padded_z, kernel):
    width = kernel.shape[-1]
    flipped = kernel.reshape(3, 3, 3, width, width)[::-1, ::-1, ::-1].transpose(0, 1, 2, 4, 3)
    return lax.conv_general_dilated(padded_z, flipped, (1, 1, 1), [(0, 0), (1, 1), (1, 1)], dimension_numbers=('NDHWC', 'DHWIO', 'NDHWC'), preferred_element_type=jnp.float32)

def weight_grad(padded_z, grad):
    width = grad.shape[-1]
    full = jnp.pad(padded_z, ((0, 0), (0, 0), (1, 1), (1, 1), (0, 0)))
    planes, rows, cols = (grad.shape[1], grad.shape[2], grad.shape[3])
    flat = grad.reshape(-1, width)
    blocks = []
    for step_z in range(3):
        for step_y in range(3):
            for step_x in range(3):
                piece = full[:, step_z:step_z + planes, step_y:step_y + rows, step_x:step_x + cols, :].reshape(-1, width)
                blocks.append(lax.dot_general(piece, flat, (((0,), (0,)), ((), ())), preferred_element_type=jnp.float32))
    return jnp.stack(blocks).reshape(-1, width)

def pad_planes(field):
    return jnp.pad(field, ((0, 0), (1, 1), (0, 0), (0, 0), (0, 0)))

def reference(layer_input, pre_act, cotangent, w_one, w_two):
    factor = 1.0 / math.sqrt(CELLS)
    pre_f = pre_act.astype(jnp.float32)
    act = jnp.where(pre_f > 0, pre_f, leak_slope * pre_f).astype(jnp.bfloat16)
    grad_two = weight_grad(pad_planes(act), cotangent) * factor
    act_grad = data_grad(pad_planes(cotangent), w_two)
    pre_grad = (act_grad * jnp.where(pre_f > 0, 1.0, leak_slope)).astype(jnp.bfloat16)
    grad_one = weight_grad(pad_planes(layer_input), pre_grad) * factor
    input_grad = data_grad(pad_planes(pre_grad), w_one).astype(jnp.bfloat16)
    return (input_grad, grad_one, grad_two)
```

```python
import functools
import math

import jax
import jax.numpy as jnp
from jax import lax
from jax.experimental import pallas as pl
from jax.experimental.pallas import tpu as pltpu
from jax.sharding import PartitionSpec as P

leak_slope = 0.3
MESH = pl.DeviceIdType.MESH
BF = jnp.bfloat16
F32 = jnp.float32

CH = 128
ROW = 16
EDGE = 32
PLANE = EDGE * ROW
PAD = PLANE + 2 * ROW
PART = PLANE // 8


def remote(src, dst, ssem, rsem, dev):
    return pltpu.make_async_remote_copy(
        src_ref=src, dst_ref=dst, send_sem=ssem, recv_sem=rsem, device_id=dev, device_id_type=MESH
    )


class Halo:
    def __init__(self, rep, g, low, high, halo, relay, ss, rs):
        self.rep, self.g = rep, g
        self.far = lax.rem(rep + 32, 64)
        self.low, self.high, self.halo, self.relay, self.ss, self.rs = low, high, halo, relay, ss, rs

    def up(self):
        return remote(self.high, self.halo.at[0], self.ss.at[0], self.rs.at[0], (self.rep, self.g + 1))

    def down(self):
        return remote(self.low, self.halo.at[1], self.ss.at[1], self.rs.at[1], (self.rep, self.g - 1))

    def part(self, side, k):
        src = self.high if side == 0 else self.low
        return remote(
            src.at[pl.ds(k * PART, PART)],
            self.relay.at[side],
            self.ss.at[2 + k],
            self.rs.at[2 + side],
            (self.far, k),
        )

    def pass_on(self, side):
        return remote(
            self.relay.at[side],
            self.halo.at[side, pl.ds(pl.multiple_of(self.g * PART, PART), PART)],
            self.ss.at[10 + side],
            self.rs.at[4 + self.g],
            (self.far, 4 - side),
        )

    def landed(self, side, k):
        block = self.halo.at[side, pl.ds(k * PART, PART)]
        return remote(block, block, self.ss.at[2 + k], self.rs.at[4 + k], (self.far, k))

    def send_high(self):
        @pl.when((self.g != 3) & (self.g != 7))
        def _():
            self.up().start()

        @pl.when(self.g == 3)
        def _():
            for k in range(8):
                self.part(0, k).start()

    def send_low(self):
        @pl.when((self.g != 0) & (self.g != 4))
        def _():
            self.down().start()

        @pl.when(self.g == 4)
        def _():
            for k in range(8):
                self.part(1, k).start()

    def forward(self):
        for side in (0, 1):
            copy = remote(
                self.relay.at[side], self.relay.at[side], self.ss.at[10], self.rs.at[2 + side], (self.far, 3)
            )
            copy.wait_recv()
            self.pass_on(side).start()

    def wait_low(self):
        @pl.when((self.g != 0) & (self.g != 4))
        def _():
            self.up().wait_recv()

        @pl.when(self.g == 4)
        def _():
            for k in range(8):
                self.landed(0, k).wait_recv()

    def wait_high(self):
        @pl.when((self.g != 3) & (self.g != 7))
        def _():
            self.down().wait_recv()

        @pl.when(self.g == 3)
        def _():
            for k in range(8):
                self.landed(1, k).wait_recv()

    def drain(self):
        @pl.when((self.g != 3) & (self.g != 7))
        def _():
            self.up().wait_send()

        @pl.when((self.g != 0) & (self.g != 4))
        def _():
            self.down().wait_send()

        @pl.when(self.g == 3)
        def _():
            for k in range(8):
                self.part(0, k).wait_send()

        @pl.when(self.g == 4)
        def _():
            for k in range(8):
                self.part(1, k).wait_send()

        for side in (0, 1):
            self.pass_on(side).wait_send()


class Where:
    def __init__(self):
        self.rep, self.g = lax.axis_index("rep"), lax.axis_index("gz")
        self.core = lax.rem(self.rep, 2)
        self.x = lax.rem(lax.div(self.rep, 2), 4)
        self.zl = lax.div(self.rep, 8)
        self.y = lax.rem(self.g, 4)
        self.zh = lax.div(self.g, 4)
        self.z = self.zh * 8 + self.zl

    def other_core(self):
        return (self.rep + 1 - 2 * self.core, self.g)

    def at_x(self, d):
        x = lax.rem(self.x + d, 4)
        return x, (self.zl * 8 + x * 2 + self.core, self.g)

    def at_y(self, d):
        y = lax.rem(self.y + d, 4)
        return y, (self.rep, self.zh * 4 + y)

    def at_z(self, d):
        z = lax.rem(self.z + d, 16)
        rest = self.rep - self.zl * 8
        return z, (lax.rem(z, 8) * 8 + rest, lax.div(z, 8) * 4 + self.y)


class Reduce:
    def __init__(self, w, s, rc, t, r1, u, r2, zs, rz, ss, rs):
        self.w = w
        self.s, self.rc, self.t, self.r1, self.u = s, rc, t, r1, u
        self.r2, self.zs, self.rz, self.ss, self.rs = r2, zs, rz, ss, rs

    def core_copy(self):
        return remote(
            self.s.at[1 - self.w.core], self.rc, self.ss.at[0], self.rs.at[0], self.w.other_core()
        )

    def first(self, half, d):
        place, dev = self.w.at_x(d) if half == 0 else self.w.at_y(d)
        k = 1 + half * 3 + d - 1
        return remote(self.t.at[half, place], self.r1.at[half, d - 1], self.ss.at[k], self.rs.at[k], dev)

    def second(self, half, d):
        place, dev = self.w.at_y(d) if half == 0 else self.w.at_x(d)
        k = 7 + half * 3 + d - 1
        return remote(self.u.at[half, place], self.r2.at[half, d - 1], self.ss.at[k], self.rs.at[k], dev)

    def last(self, d):
        place, dev = self.w.at_z(d)
        k = 13 + d - 1
        return remote(self.zs.at[place], self.rz.at[d - 1], self.ss.at[k], self.rs.at[k], dev)

    def start(self):
        self.core_copy().start()

    def step_core(self):
        self.core_copy().wait_recv()
        core = self.w.core
        for half in range(2):

            def body(i, carry):
                for j in range(4):
                    own = self.s[core, half, i, j].astype(F32)
                    self.t[half, i, j] = (own + self.rc[half, i, j].astype(F32)).astype(BF)
                return carry

            lax.fori_loop(0, 4, body, 0)
            for d in (2, 1, 3):
                self.first(half, d).start()

    def step_first(self):
        for half in range(2):
            mine = self.w.x if half == 0 else self.w.y
            for d in (1, 3, 2):
                self.first(half, d).wait_recv()

            def body(i, carry):
                total = self.t[half, mine, i].astype(F32)
                for k in range(3):
                    total += self.r1[half, k, i].astype(F32)
                self.u[half, i] = total.astype(BF)
                return carry

            lax.fori_loop(0, 4, body, 0)
            for d in (2, 1, 3):
                self.second(half, d).start()

    def step_second(self):
        for half in range(2):
            mine = self.w.y if half == 0 else self.w.x
            for d in (1, 3, 2):
                self.second(half, d).wait_recv()
            total = self.u[half, mine].astype(F32)
            for k in range(3):
                total += self.r2[half, k].astype(F32)
            self.zs[half * 8 : half * 8 + 8] = total.reshape(8, 8, CH)
        for d in (8, 7, 9, 6, 10, 5, 11, 4, 12, 3, 13, 2, 14, 1, 15):
            self.last(d).start()

    def finish(self, out, factor):
        total = self.zs[self.w.z]
        for d in (1, 15, 2, 14, 3, 13, 4, 12, 5, 11, 6, 10, 7, 9, 8):
            self.last(d).wait_recv()
            total += self.rz[d - 1]
        total = total * factor
        for q in range(8):
            piece = total if q == 0 else pltpu.roll(total, CH - 16 * q, 1)
            rows = 7 if q < 7 else 5
            out[7 * q : 7 * q + rows, :] = piece[:rows, :16]

    def drain(self):
        self.core_copy().wait_send()
        for half in range(2):
            for d in (1, 2, 3):
                self.first(half, d).wait_send()
                self.second(half, d).wait_send()
        for d in range(1, 16):
            self.last(d).wait_send()


def regroup(flat, s):
    group = lax.broadcasted_iota(jnp.int32, (8, CH), 1)
    masks = {b: lax.rem(lax.div(group, 16 * b), 2) == 1 for b in (1, 2, 4)}

    def body(pair, carry):
        block = flat.at[pl.ds(pl.multiple_of(pair * 864, 8), 872)]
        for x in range(4):
            for core in range(2):
                tiles = []
                for odd in range(2):
                    base = odd * 432 + x * 108 + core * 54
                    v = [block[base + 7 * q : base + 7 * q + 8, :] for q in range(8)]
                    for b in (1, 2, 4):
                        for q in range(8):
                            if q & b:
                                continue
                            a, c = v[q], v[q | b]
                            v[q] = jnp.where(masks[b], pltpu.roll(c, 16 * b, 1), a)
                            v[q | b] = jnp.where(masks[b], c, pltpu.roll(a, CH - 16 * b, 1))
                    tiles.append(v)
                rows = pl.ds(pl.multiple_of(pair * 16, 16), 16)
                for q in range(8):
                    both = jnp.concatenate([tiles[0][q], tiles[1][q]], axis=0).astype(BF)
                    if q < 4:
                        s[core, 0, x, q, rows, :] = both
                    else:
                        s[core, 1, q - 4, x, rows, :] = both
        return carry

    lax.fori_loop(0, 4, body, 0)


def spread(plane, ext, at):
    wide = plane.astype(F32)
    col = lax.rem(lax.broadcasted_iota(jnp.int32, (PLANE, CH), 0), ROW)
    before = jnp.where(col == 0, 0.0, pltpu.roll(wide, 1, 0)).astype(BF)
    after = jnp.where(col == ROW - 1, 0.0, pltpu.roll(wide, PLANE - 1, 0)).astype(BF)
    rows = slice(ROW, ROW + PLANE)
    ext[at, rows, 0:CH] = before
    ext[at, rows, CH : 2 * CH] = plane
    ext[at, rows, 2 * CH : 3 * CH] = after


def slabs(ext, at):
    return jnp.concatenate([ext[at, dy * ROW : dy * ROW + PLANE, :] for dy in range(3)], axis=1)


def mm(a, b):
    return jnp.dot(a, b, preferred_element_type=F32)


def lay_weights(w, wt):
    for a in range(3):
        for dy in range(3):
            for dx in range(3):
                k = dy * 3 + dx
                wt[a, k * CH : (k + 1) * CH, :] = w[9 * a + 8 - k].T


def inner_data_grad(ext, wt, acc):
    for at in (1, 2):
        x = slabs(ext, at)
        pair = jnp.concatenate([wt[2 - at], wt[3 - at]], axis=1)
        if at == 1:
            acc[...] = mm(x, pair)
        else:
            acc[...] += mm(x, pair)


def kernel(
    factor, li_h, pa_h, ct_h, w1_h, w2_h, ig, g1, g2,
    li, pa, ct, w1, w2, ct_halo, li_halo, pg_halo, ct_relay, li_relay, pg_relay,
    e_ct, e_pg, pg, act_t, li_t, wt2, wt1, acc, flat,
    s1, rc1, t1, r11, u1, r21, zs1, rz1, s2, rc2, t2, r12, u2, r22, zs2, rz2,
    in_sem, hs_ct, hr_ct, hs_li, hr_li, hs_pg, hr_pg, ss1, rs1, ss2, rs2,
):
    w = Where()
    rep, g = w.rep, w.g
    loads = [
        pltpu.make_async_copy(a, b, in_sem.at[k])
        for k, (a, b) in enumerate([(ct_h, ct), (w2_h, w2), (pa_h, pa), (li_h, li), (w1_h, w1)])
    ]
    for load in loads:
        load.start()

    barrier = pltpu.get_barrier_semaphore()
    peers = [w.other_core()]
    peers += [w.at_x(d)[1] for d in (1, 2, 3)] + [w.at_y(d)[1] for d in (1, 2, 3)]
    peers += [w.at_z(d)[1] for d in range(1, 16)]
    far = lax.rem(rep + 32, 64)
    peers += [(far, 3), (far, 4)]
    for dev in peers:
        pl.semaphore_signal(barrier, inc=1, device_id=dev, device_id_type=MESH)
    middle = (g == 3) | (g == 4)

    @pl.when(middle)
    def _():
        for k in range(8):
            pl.semaphore_signal(barrier, inc=1, device_id=(far, k), device_id_type=MESH)

    @pl.when(middle)
    def _():
        pl.semaphore_wait(barrier, len(peers) + 8)

    @pl.when(jnp.logical_not(middle))
    def _():
        pl.semaphore_wait(barrier, len(peers))

    low, high = pl.ds(0, PLANE), pl.ds(PLANE, PLANE)
    loads[0].wait()
    h_ct = Halo(rep, g, ct.at[low], ct.at[high], ct_halo, ct_relay, hs_ct, hr_ct)
    h_ct.send_high()
    h_ct.send_low()
    loads[3].wait()
    h_li = Halo(rep, g, li.at[low], li.at[high], li_halo, li_relay, hs_li, hr_li)
    h_li.send_high()
    h_li.send_low()
    h_pg = Halo(rep, g, pg.at[low], pg.at[high], pg_halo, pg_relay, hs_pg, hr_pg)

    @pl.when(g == 0)
    def _():
        for halo in (ct_halo, li_halo, pg_halo):
            halo[0] = jnp.zeros((PLANE, CH), BF)

    @pl.when(g == 7)
    def _():
        for halo in (ct_halo, li_halo, pg_halo):
            halo[1] = jnp.zeros((PLANE, CH), BF)

    edge = jnp.zeros((4, ROW, 3 * CH), BF)
    for ext in (e_ct, e_pg):
        ext[:, 0:ROW, :] = edge
        ext[:, ROW + PLANE : PAD, :] = edge
    flat[27 * CH : 27 * CH + 8, :] = jnp.zeros((8, CH), F32)
    spread(ct[low, :], e_ct, 1)
    spread(ct[high, :], e_ct, 2)
    loads[1].wait()
    lay_weights(w2, wt2)
    h_ct.forward()
    inner_data_grad(e_ct, wt2, acc)
    loads[2].wait()
    for q in range(2):
        v = pa[q * PLANE : (q + 1) * PLANE, :].astype(F32)
        act = jnp.where(v > 0, v, leak_slope * v).astype(BF)
        act_t[:, q * PLANE : (q + 1) * PLANE] = act.T
    h_li.forward()

    h_ct.wait_low()
    spread(ct_halo[0], e_ct, 0)
    h_ct.wait_high()
    spread(ct_halo[1], e_ct, 3)
    for q in range(2):
        total = acc[:, q * CH : (q + 1) * CH] + mm(slabs(e_ct, 3 * q), wt2[2 - 2 * q])
        rows = pl.ds(q * PLANE, PLANE)
        v = pa[rows, :].astype(F32)
        pg[rows, :] = (total * jnp.where(v > 0, 1.0, leak_slope)).astype(BF)
        if q == 0:
            h_pg.send_low()
        else:
            h_pg.send_high()

    order = [(0, 1), (2, 3), (4, 5), (6, 7), (8,)]

    def taps(ext, at, group):
        parts = []
        for k in group:
            dy, dx = 2 - k // 3, 2 - k % 3
            parts.append(ext[at, dy * ROW : dy * ROW + PLANE, dx * CH : (dx + 1) * CH])
        return parts[0] if len(parts) == 1 else jnp.concatenate(parts, axis=1)

    a0, a1 = act_t[:, 0:PLANE], act_t[:, PLANE : 2 * PLANE]
    for group in order:
        e = [taps(e_ct, at, group) for at in range(4)]
        mid = mm(jnp.concatenate([a0, a1], axis=0), e[1])
        after = mm(jnp.concatenate([a0, a1], axis=0), e[2])
        planes = [
            after[:CH] + mm(a1, e[3]),
            mid[:CH] + after[CH:],
            mid[CH:] + mm(a0, e[0]),
        ]
        for a in range(3):
            for j, k in enumerate(group):
                t = 9 * a + k
                flat[t * CH : (t + 1) * CH, :] = planes[a][:, j * CH : (j + 1) * CH]
    red2 = Reduce(w, s2, rc2, t2, r12, u2, r22, zs2, rz2, ss2, rs2)
    regroup(flat, s2)
    red2.start()
    h_pg.forward()

    spread(pg[low, :], e_pg, 1)
    spread(pg[high, :], e_pg, 2)
    li_t[:, PLANE : 2 * PLANE] = li[low, :].T
    li_t[:, 2 * PLANE : 3 * PLANE] = li[high, :].T
    h_li.wait_low()
    li_t[:, 0:PLANE] = li_halo[0].T
    h_li.wait_high()
    li_t[:, 3 * PLANE : 4 * PLANE] = li_halo[1].T
    red2.step_core()
    for group in order:
        total = None
        for at in (1, 2):
            lhs = jnp.concatenate(
                [li_t[:, (at + a - 1) * PLANE : (at + a) * PLANE] for a in range(3)], axis=0
            )
            term = mm(lhs, taps(e_pg, at, group))
            total = term if total is None else total + term
        for a in range(3):
            for j, k in enumerate(group):
                t = 9 * a + k
                flat[t * CH : (t + 1) * CH, :] = total[a * CH : (a + 1) * CH, j * CH : (j + 1) * CH]
    red1 = Reduce(w, s1, rc1, t1, r11, u1, r21, zs1, rz1, ss1, rs1)
    regroup(flat, s1)
    red1.start()
    red2.step_first()

    loads[4].wait()
    lay_weights(w1, wt1)
    red1.step_core()
    red2.step_second()
    inner_data_grad(e_pg, wt1, acc)
    h_pg.wait_low()
    spread(pg_halo[0], e_pg, 0)
    h_pg.wait_high()
    spread(pg_halo[1], e_pg, 3)
    red1.step_first()
    red2.finish(g2, factor)
    for q in range(2):
        total = acc[:, q * CH : (q + 1) * CH] + mm(slabs(e_pg, 3 * q), wt1[2 - 2 * q])
        ig[q * PLANE : (q + 1) * PLANE, :] = total.astype(BF)
        if q == 0:
            red1.step_second()
    red1.finish(g1, factor)

    for halo in (h_ct, h_li, h_pg):
        halo.drain()
    red2.drain()
    red1.drain()


def reduce_buffers():
    return [
        pltpu.VMEM((2, 2, 4, 4, 64, CH), BF),
        pltpu.VMEM((2, 4, 4, 64, CH), BF),
        pltpu.VMEM((2, 4, 4, 64, CH), BF),
        pltpu.VMEM((2, 3, 4, 64, CH), BF),
        pltpu.VMEM((2, 4, 64, CH), BF),
        pltpu.VMEM((2, 3, 64, CH), BF),
        pltpu.VMEM((16, 8, CH), F32),
        pltpu.VMEM((15, 8, CH), F32),
    ]


def on_device(layer_input, pre_act, cotangent, w_one, w_two):
    shape = layer_input.shape
    cells = 2 * PLANE
    factor = 1.0 / math.sqrt(cells * lax.axis_size("rep") * lax.axis_size("gz"))
    flat_in = [v.reshape(cells, CH) for v in (layer_input, pre_act, cotangent)]
    any_spec = pl.BlockSpec(memory_space=pl.ANY)
    vmem_spec = pl.BlockSpec(memory_space=pltpu.VMEM)
    dma = pltpu.SemaphoreType.DMA
    field = pltpu.VMEM((cells, CH), BF)
    kern = pltpu.VMEM((27, CH, CH), BF)
    halo = pltpu.VMEM((2, PLANE, CH), BF)
    relay = pltpu.VMEM((2, PART, CH), BF)
    ext = pltpu.VMEM((4, PAD, 3 * CH), BF)
    turned = pltpu.VMEM((3, 9 * CH, CH), BF)
    input_grad, grad_one, grad_two = pl.pallas_call(
        functools.partial(kernel, factor),
        out_shape=(
            jax.ShapeDtypeStruct((cells, CH), BF),
            jax.ShapeDtypeStruct((54, 16), F32),
            jax.ShapeDtypeStruct((54, 16), F32),
        ),
        in_specs=[any_spec] * 5,
        out_specs=(vmem_spec, vmem_spec, vmem_spec),
        scratch_shapes=[
            field, field, field, kern, kern, halo, halo, halo, relay, relay, relay,
            ext, ext, field, pltpu.VMEM((CH, cells), BF), pltpu.VMEM((CH, 2 * cells), BF),
            turned, turned, pltpu.VMEM((PLANE, 2 * CH), F32), pltpu.VMEM((27 * CH + 8, CH), F32),
            *reduce_buffers(), *reduce_buffers(),
            dma((5,)), *[dma((12,))] * 6, *[dma((28,))] * 4,
        ],
        compiler_params=pltpu.CompilerParams(
            collective_id=0, has_side_effects=True, vmem_limit_bytes=48 * 2**20
        ),
    )(*flat_in, w_one, w_two)
    return (input_grad.reshape(shape), grad_one, grad_two)


def solution(mesh):
    cells = P("rep", "gz", None, None, None)
    return jax.shard_map(
        on_device,
        mesh=mesh,
        in_specs=(cells, cells, cells, P(), P()),
        out_specs=(cells, P("rep", "gz"), P("rep", "gz")),
        check_vma=False,
    )
```

```python
import functools
import math

import jax
import jax.numpy as jnp
from jax import lax
from jax.experimental import pallas as pl
from jax.experimental.pallas import tpu as pltpu
from jax.sharding import PartitionSpec as P

leak_slope = 0.3
MESH = pl.DeviceIdType.MESH
BF = jnp.bfloat16
F32 = jnp.float32

CH = 128
ROW = 16
EDGE = 32
PLANE = EDGE * ROW
PAD = PLANE + 2 * ROW
PART = PLANE // 4


def remote(src, dst, ssem, rsem, dev):
    return pltpu.make_async_remote_copy(
        src_ref=src, dst_ref=dst, send_sem=ssem, recv_sem=rsem, device_id=dev, device_id_type=MESH
    )


class Halo:
    def __init__(self, rep, g, low, high, halo, relay, ss, rs):
        self.rep, self.g = rep, g
        self.low, self.high, self.halo, self.relay, self.ss, self.rs = low, high, halo, relay, ss, rs

    def up(self):
        return remote(self.high, self.halo.at[0], self.ss.at[0], self.rs.at[0], (self.rep, self.g + 1))

    def down(self):
        return remote(self.low, self.halo.at[1], self.ss.at[1], self.rs.at[1], (self.rep, self.g - 1))

    def parts(self, side):
        src, home, first = (self.high, 3, 0) if side == 0 else (self.low, 0, 4)
        copies = []
        for k in range(4):
            rows = pl.ds(k * PART, PART)
            if k == home:
                dst, sem, dev = self.halo.at[side, rows], self.rs.at[3 + k], (self.rep, 4 - side)
            else:
                dst, sem, dev = self.relay, self.rs.at[2], (self.rep, first + k)
            copies.append(remote(src.at[rows], dst, self.ss.at[2 + k], sem, dev))
        return copies

    def pass_on(self, side):
        k = self.g if side == 0 else self.g - 4
        return remote(
            self.relay,
            self.halo.at[side, pl.ds(pl.multiple_of(k * PART, PART), PART)],
            self.ss.at[6],
            self.rs.at[3 + k],
            (self.rep, 4 - side),
        )

    def landed(self, side, k):
        block = self.halo.at[side, pl.ds(k * PART, PART)]
        return remote(block, block, self.ss.at[2 + k], self.rs.at[3 + k], (self.rep, 3 + side))

    def send_high(self):
        @pl.when((self.g != 3) & (self.g != 7))
        def _():
            self.up().start()

        @pl.when(self.g == 3)
        def _():
            for copy in self.parts(0):
                copy.start()

    def send_low(self):
        @pl.when((self.g != 0) & (self.g != 4))
        def _():
            self.down().start()

        @pl.when(self.g == 4)
        def _():
            for copy in self.parts(1):
                copy.start()

    def send(self):
        @pl.when(self.g == 4)
        def _():
            for copy in self.parts(1):
                copy.start()

        self.send_high()

        @pl.when((self.g != 0) & (self.g != 4))
        def _():
            self.down().start()

    def forward(self):
        for side, inside in ((0, self.g < 3), (1, self.g > 4)):

            @pl.when(inside)
            def _():
                copy = self.pass_on(side)
                remote(self.relay, self.relay, self.ss.at[6], self.rs.at[2], (self.rep, 4 - side)).wait_recv()
                copy.start()

    def wait_low(self):
        @pl.when((self.g != 0) & (self.g != 4))
        def _():
            self.up().wait_recv()

        @pl.when(self.g == 4)
        def _():
            for k in range(4):
                self.landed(0, k).wait_recv()

    def wait_high(self):
        @pl.when((self.g != 3) & (self.g != 7))
        def _():
            self.down().wait_recv()

        @pl.when(self.g == 3)
        def _():
            for k in range(4):
                self.landed(1, k).wait_recv()

    def drain(self):
        @pl.when((self.g != 3) & (self.g != 7))
        def _():
            self.up().wait_send()

        @pl.when((self.g != 0) & (self.g != 4))
        def _():
            self.down().wait_send()

        @pl.when(self.g == 3)
        def _():
            for copy in self.parts(0):
                copy.wait_send()

        @pl.when(self.g == 4)
        def _():
            for copy in self.parts(1):
                copy.wait_send()

        for side, inside in ((0, self.g < 3), (1, self.g > 4)):

            @pl.when(inside)
            def _():
                self.pass_on(side).wait_send()


class Where:
    def __init__(self):
        self.rep, self.g = lax.axis_index("rep"), lax.axis_index("gz")
        self.core = lax.rem(self.rep, 2)
        self.x = lax.rem(lax.div(self.rep, 2), 4)
        self.zl = lax.div(self.rep, 8)
        self.y = lax.rem(self.g, 4)
        self.zh = lax.div(self.g, 4)
        self.z = self.zh * 8 + self.zl

    def other_core(self):
        return (self.rep + 1 - 2 * self.core, self.g)

    def at_x(self, d):
        x = lax.rem(self.x + d, 4)
        return x, (self.zl * 8 + x * 2 + self.core, self.g)

    def at_y(self, d):
        y = lax.rem(self.y + d, 4)
        return y, (self.rep, self.zh * 4 + y)

    def at_z(self, d):
        z = lax.rem(self.z + d, 16)
        rest = self.rep - self.zl * 8
        return z, (lax.rem(z, 8) * 8 + rest, lax.div(z, 8) * 4 + self.y)


class Reduce:
    def __init__(self, w, s, rc, t, r1, u, r2, zs, rz, ss, rs):
        self.w = w
        self.s, self.rc, self.t, self.r1, self.u = s, rc, t, r1, u
        self.r2, self.zs, self.rz, self.ss, self.rs = r2, zs, rz, ss, rs

    def core_copy(self):
        return remote(
            self.s.at[1 - self.w.core], self.rc, self.ss.at[0], self.rs.at[0], self.w.other_core()
        )

    def first(self, half, d):
        place, dev = self.w.at_x(d) if half == 0 else self.w.at_y(d)
        k = 1 + half * 3 + d - 1
        return remote(self.t.at[half, place], self.r1.at[half, d - 1], self.ss.at[k], self.rs.at[k], dev)

    def second(self, half, d):
        place, dev = self.w.at_y(d) if half == 0 else self.w.at_x(d)
        k = 7 + half * 3 + d - 1
        return remote(self.u.at[half, place], self.r2.at[half, d - 1], self.ss.at[k], self.rs.at[k], dev)

    def last(self, d):
        place, dev = self.w.at_z(d)
        k = 13 + d - 1
        return remote(self.zs.at[place], self.rz.at[d - 1], self.ss.at[k], self.rs.at[k], dev)

    def start(self):
        self.core_copy().start()

    def step_core(self):
        self.core_copy().wait_recv()
        core = self.w.core
        for half in range(2):

            def body(i, carry):
                for j in range(4):
                    own = self.s[core, half, i, j].astype(F32)
                    self.t[half, i, j] = (own + self.rc[half, i, j].astype(F32)).astype(BF)
                return carry

            lax.fori_loop(0, 4, body, 0)
            for d in (2, 1, 3):
                self.first(half, d).start()

    def step_first(self):
        for half in range(2):
            mine = self.w.x if half == 0 else self.w.y
            for d in (1, 3, 2):
                self.first(half, d).wait_recv()

            def body(i, carry):
                total = self.t[half, mine, i].astype(F32)
                for k in range(3):
                    total += self.r1[half, k, i].astype(F32)
                self.u[half, i] = total.astype(BF)
                return carry

            lax.fori_loop(0, 4, body, 0)
            for d in (2, 1, 3):
                self.second(half, d).start()

    def step_second(self):
        for half in range(2):
            mine = self.w.y if half == 0 else self.w.x
            for d in (1, 3, 2):
                self.second(half, d).wait_recv()
            total = self.u[half, mine].astype(F32)
            for k in range(3):
                total += self.r2[half, k].astype(F32)
            self.zs[half * 8 : half * 8 + 8] = total.reshape(8, 8, CH)
        for d in (8, 7, 9, 6, 10, 5, 11, 4, 12, 3, 13, 2, 14, 1, 15):
            self.last(d).start()

    def finish(self, out, factor):
        total = self.zs[self.w.z]
        for d in (1, 15, 2, 14, 3, 13, 4, 12, 5, 11, 6, 10, 7, 9, 8):
            self.last(d).wait_recv()
            total += self.rz[d - 1]
        out[...] = total * factor

    def drain(self):
        self.core_copy().wait_send()
        for half in range(2):
            for d in (1, 2, 3):
                self.first(half, d).wait_send()
                self.second(half, d).wait_send()
        for d in range(1, 16):
            self.last(d).wait_send()


def regroup(flat, s):
    group = lax.broadcasted_iota(jnp.int32, (16, CH), 1)
    masks = {b: lax.rem(lax.div(group, 16 * b), 2) == 1 for b in (1, 2, 4)}

    def body(pair, carry):
        block = flat.at[pl.ds(pl.multiple_of(pair * 864, 8), 872)]
        rows = pl.ds(pl.multiple_of(pair * 16, 16), 16)
        for x in range(4):
            for core in range(2):
                base = x * 108 + core * 54
                v = []
                for q in range(8):
                    at = base + 7 * q
                    both = jnp.concatenate([block[at : at + 8, :], block[at + 432 : at + 440, :]], axis=0)
                    v.append(both.astype(BF))
                for b in (1, 2, 4):
                    for q in range(8):
                        if q & b:
                            continue
                        a, c = v[q], v[q | b]
                        v[q] = jnp.where(masks[b], pltpu.roll(c, 16 * b, 1), a)
                        v[q | b] = jnp.where(masks[b], c, pltpu.roll(a, CH - 16 * b, 1))
                for q in range(8):
                    if q < 4:
                        s[core, 0, x, q, rows, :] = v[q]
                    else:
                        s[core, 1, q - 4, x, rows, :] = v[q]
        return carry

    lax.fori_loop(0, 4, body, 0)


def spread(plane, ext, at):
    wide = plane.astype(F32)
    col = lax.rem(lax.broadcasted_iota(jnp.int32, (PLANE, CH), 0), ROW)
    before = jnp.where(col == 0, 0.0, pltpu.roll(wide, 1, 0)).astype(BF)
    after = jnp.where(col == ROW - 1, 0.0, pltpu.roll(wide, PLANE - 1, 0)).astype(BF)
    rows = slice(ROW, ROW + PLANE)
    ext[at, rows, 0:CH] = before
    ext[at, rows, CH : 2 * CH] = plane
    ext[at, rows, 2 * CH : 3 * CH] = after


def slabs(ext, at):
    return jnp.concatenate([ext[at, dy * ROW : dy * ROW + PLANE, :] for dy in range(3)], axis=1)


def mm(a, b):
    return jnp.dot(a, b, preferred_element_type=F32)


def lay_weights(w, wt):
    for a in range(3):
        for dy in range(3):
            for dx in range(3):
                k = dy * 3 + dx
                wt[a, k * CH : (k + 1) * CH, :] = w[9 * a + 8 - k].T


def inner_data_grad(ext, wt, acc):
    for at in (1, 2):
        x = slabs(ext, at)
        pair = jnp.concatenate([wt[2 - at], wt[3 - at]], axis=1)
        if at == 1:
            acc[...] = mm(x, pair)
        else:
            acc[...] += mm(x, pair)


def kernel(
    factor, li_h, pa_h, ct_h, w1_h, w2_h, ig, tiles,
    li, pa, ct, w1, w2, ig_v, ct_halo, li_halo, pg_halo, ct_relay, li_relay, pg_relay,
    e_ct, e_pg, pg, act_t, li_t, wt2, wt1, acc, flat1, flat2,
    s1, rc1, t1, r11, u1, r21, zs1, rz1, s2, rc2, t2, r12, u2, r22, zs2, rz2,
    in_sem, hs_ct, hr_ct, hs_li, hr_li, hs_pg, hr_pg, ss1, rs1, ss2, rs2,
):
    w = Where()
    rep, g = w.rep, w.g
    loads = [
        pltpu.make_async_copy(a, b, in_sem.at[k])
        for k, (a, b) in enumerate([(ct_h, ct), (w2_h, w2), (pa_h, pa), (li_h, li), (w1_h, w1)])
    ]
    for load in loads:
        load.start()

    barrier = pltpu.get_barrier_semaphore()
    peers = [w.other_core()]
    peers += [w.at_x(d)[1] for d in (1, 2, 3)] + [w.at_y(d)[1] for d in (1, 2, 3)]
    peers += [w.at_z(d)[1] for d in range(1, 16)]
    for dev in peers:
        pl.semaphore_signal(barrier, inc=1, device_id=dev, device_id_type=MESH)
    for end, senders in ((3, (4, 5, 6)), (4, (1, 2, 3))):

        @pl.when(g == end)
        def _():
            for k in senders:
                pl.semaphore_signal(barrier, inc=1, device_id=(rep, k), device_id_type=MESH)

    @pl.when(g == 0)
    def _():
        for halo in (ct_halo, li_halo, pg_halo):
            halo[0] = jnp.zeros((PLANE, CH), BF)

    @pl.when(g == 7)
    def _():
        for halo in (ct_halo, li_halo, pg_halo):
            halo[1] = jnp.zeros((PLANE, CH), BF)

    edge = jnp.zeros((4, ROW, 3 * CH), BF)
    for ext in (e_ct, e_pg):
        ext[:, 0:ROW, :] = edge
        ext[:, ROW + PLANE : PAD, :] = edge
    for flat in (flat1, flat2):
        flat[27 * CH : 27 * CH + 8, :] = jnp.zeros((8, CH), F32)
    loads[0].wait()

    between = (g > 0) & (g < 7)

    @pl.when(between)
    def _():
        pl.semaphore_wait(barrier, len(peers) + 1)

    @pl.when(jnp.logical_not(between))
    def _():
        pl.semaphore_wait(barrier, len(peers))

    low, high = pl.ds(0, PLANE), pl.ds(PLANE, PLANE)
    h_ct = Halo(rep, g, ct.at[low], ct.at[high], ct_halo, ct_relay, hs_ct, hr_ct)
    h_li = Halo(rep, g, li.at[low], li.at[high], li_halo, li_relay, hs_li, hr_li)
    h_pg = Halo(rep, g, pg.at[low], pg.at[high], pg_halo, pg_relay, hs_pg, hr_pg)
    red1 = Reduce(w, s1, rc1, t1, r11, u1, r21, zs1, rz1, ss1, rs1)
    red2 = Reduce(w, s2, rc2, t2, r12, u2, r22, zs2, rz2, ss2, rs2)
    h_ct.send()
    spread(ct[low, :], e_ct, 1)
    spread(ct[high, :], e_ct, 2)
    loads[1].wait()
    lay_weights(w2, wt2)
    h_ct.forward()
    loads[3].wait()
    h_li.send()
    inner_data_grad(e_ct, wt2, acc)
    loads[2].wait()
    for q in range(2):
        v = pa[q * PLANE : (q + 1) * PLANE, :].astype(F32)
        act = jnp.where(v > 0, v, leak_slope * v).astype(BF)
        act_t[:, q * PLANE : (q + 1) * PLANE] = act.T
    li_t[:, PLANE : 2 * PLANE] = li[low, :].T
    li_t[:, 2 * PLANE : 3 * PLANE] = li[high, :].T
    h_li.forward()

    order = [(0, 1), (2, 3), (4, 5), (6, 7), (8,)]

    def taps(ext, at, group):
        parts = []
        for k in group:
            dy, dx = 2 - k // 3, 2 - k % 3
            parts.append(ext[at, dy * ROW : dy * ROW + PLANE, dx * CH : (dx + 1) * CH])
        return parts[0] if len(parts) == 1 else jnp.concatenate(parts, axis=1)

    def put(flat, group, a, value, more=False):
        for j, k in enumerate(group):
            t = 9 * a + k
            rows = slice(t * CH, (t + 1) * CH)
            tap = value[:, j * CH : (j + 1) * CH]
            flat[rows, :] = flat[rows, :] + tap if more else tap

    a0, a1 = act_t[:, 0:PLANE], act_t[:, PLANE : 2 * PLANE]
    for group in order:
        stack = jnp.concatenate([a0, a1], axis=0)
        mid = mm(stack, taps(e_ct, 1, group))
        after = mm(stack, taps(e_ct, 2, group))
        put(flat2, group, 0, after[:CH])
        put(flat2, group, 1, mid[:CH] + after[CH:])
        put(flat2, group, 2, mid[CH:])
    loads[4].wait()
    lay_weights(w1, wt1)

    for q in range(2):
        if q == 0:
            h_ct.wait_low()
        else:
            h_ct.wait_high()
        spread(ct_halo[q], e_ct, 3 * q)
        total = acc[:, q * CH : (q + 1) * CH] + mm(slabs(e_ct, 3 * q), wt2[2 - 2 * q])
        rows = pl.ds(q * PLANE, PLANE)
        v = pa[rows, :].astype(F32)
        pg[rows, :] = (total * jnp.where(v > 0, 1.0, leak_slope)).astype(BF)
        if q == 0:
            h_pg.send_low()
        else:
            h_pg.send_high()

    def edge_two():
        for group in order:
            put(flat2, group, 0, mm(a1, taps(e_ct, 3, group)), more=True)
            put(flat2, group, 2, mm(a0, taps(e_ct, 0, group)), more=True)

    def send_two():
        regroup(flat2, s2)
        red2.start()

    def spread_pg():
        spread(pg[low, :], e_pg, 1)
        spread(pg[high, :], e_pg, 2)

    def turn_li():
        h_li.wait_low()
        li_t[:, 0:PLANE] = li_halo[0].T
        h_li.wait_high()
        li_t[:, 3 * PLANE : 4 * PLANE] = li_halo[1].T

    def grad_one():
        for group in order:
            total = None
            for at in (1, 2):
                lhs = jnp.concatenate(
                    [li_t[:, (at + a - 1) * PLANE : (at + a) * PLANE] for a in range(3)], axis=0
                )
                term = mm(lhs, taps(e_pg, at, group))
                total = term if total is None else total + term
            for a in range(3):
                put(flat1, group, a, total[a * CH : (a + 1) * CH])

    def send_one():
        regroup(flat1, s1)
        red1.start()

    def inner():
        inner_data_grad(e_pg, wt1, acc)

    def pg_low():
        h_pg.wait_low()
        spread(pg_halo[0], e_pg, 0)

    def pg_high():
        h_pg.wait_high()
        spread(pg_halo[1], e_pg, 3)

    save = pltpu.make_async_copy(ig_v, ig, in_sem.at[5])

    def outer():
        for q in range(2):
            total = acc[:, q * CH : (q + 1) * CH] + mm(slabs(e_pg, 3 * q), wt1[2 - 2 * q])
            ig_v[q * PLANE : (q + 1) * PLANE, :] = total.astype(BF)
        save.start()

    steps = (edge_two, send_two, h_pg.forward, spread_pg, turn_li, grad_one, red2.step_core, send_one, inner, red1.step_core, red2.step_first, pg_low, pg_high, outer, red1.step_first, red2.step_second, red1.step_second, functools.partial(red2.finish, tiles.at[1], factor), functools.partial(red1.finish, tiles.at[0], factor))
    for step in steps:
        step()
    save.wait()

    for halo in (h_ct, h_li, h_pg):
        halo.drain()
    red2.drain()
    red1.drain()


def close(ig_in, tiles, ig, one, two, through, load_sem, save_sem):
    rows = ig_in.shape[0] // 4
    loads, saves = [], []
    for k in range(4):
        at = pl.ds(k * rows, rows)
        loads.append(pltpu.make_async_copy(ig_in.at[at], through.at[at], load_sem.at[k]))
        saves.append(pltpu.make_async_copy(through.at[at], ig.at[at], save_sem.at[k]))
        loads[k].start()
    for k in range(4):
        loads[k].wait()
        saves[k].start()
    for k, out in enumerate((one, two)):
        turned = tiles[k].T
        for q in range(8):
            rows = 7 if q < 7 else 5
            out[:, 7 * q : 7 * q + rows] = turned[16 * q : 16 * q + 16, :rows]
    for save in saves:
        save.wait()


def reduce_buffers():
    return [
        pltpu.VMEM((2, 2, 4, 4, 64, CH), BF),
        pltpu.VMEM((2, 4, 4, 64, CH), BF),
        pltpu.VMEM((2, 4, 4, 64, CH), BF),
        pltpu.VMEM((2, 3, 4, 64, CH), BF),
        pltpu.VMEM((2, 4, 64, CH), BF),
        pltpu.VMEM((2, 3, 64, CH), BF),
        pltpu.VMEM((16, 8, CH), F32),
        pltpu.VMEM((15, 8, CH), F32),
    ]


def on_device(layer_input, pre_act, cotangent, w_one, w_two):
    shape = layer_input.shape
    cells = 2 * PLANE
    factor = 1.0 / math.sqrt(cells * lax.axis_size("rep") * lax.axis_size("gz"))
    flat_in = [v.reshape(cells, CH) for v in (layer_input, pre_act, cotangent)]
    any_spec = pl.BlockSpec(memory_space=pl.ANY)
    vmem_spec = pl.BlockSpec(memory_space=pltpu.VMEM)
    dma = pltpu.SemaphoreType.DMA
    field = pltpu.VMEM((cells, CH), BF)
    kern = pltpu.VMEM((27, CH, CH), BF)
    halo = pltpu.VMEM((2, PLANE, CH), BF)
    relay = pltpu.VMEM((PART, CH), BF)
    ext = pltpu.VMEM((4, PAD, 3 * CH), BF)
    turned = pltpu.VMEM((3, 9 * CH, CH), BF)
    held, tiles = pl.pallas_call(
        functools.partial(kernel, factor),
        out_shape=(
            jax.ShapeDtypeStruct((cells, CH), BF),
            jax.ShapeDtypeStruct((2, 8, CH), F32),
        ),
        in_specs=[any_spec] * 5,
        out_specs=(any_spec, vmem_spec),
        scratch_shapes=[
            field, field, field, kern, kern, field, halo, halo, halo, relay, relay, relay,
            ext, ext, field, pltpu.VMEM((CH, cells), BF), pltpu.VMEM((CH, 2 * cells), BF),
            turned, turned, pltpu.VMEM((PLANE, 2 * CH), F32), *[pltpu.VMEM((27 * CH + 8, CH), F32)] * 2,
            *reduce_buffers(), *reduce_buffers(),
            dma((6,)), *[dma((7,))] * 6, *[dma((28,))] * 4,
        ],
        compiler_params=pltpu.CompilerParams(
            collective_id=0, has_side_effects=True, vmem_limit_bytes=62 * 2**20
        ),
    )(*flat_in, w_one, w_two)
    input_grad, one, two = pl.pallas_call(
        close,
        out_shape=(
            jax.ShapeDtypeStruct((cells, CH), BF),
            jax.ShapeDtypeStruct((16, 54), F32),
            jax.ShapeDtypeStruct((16, 54), F32),
        ),
        in_specs=[any_spec, vmem_spec],
        out_specs=(any_spec, vmem_spec, vmem_spec),
        scratch_shapes=[field, dma((4,)), dma((4,))],
    )(held, tiles)
    return (input_grad.reshape(shape), one.T, two.T)


def solution(mesh):
    cells = P("rep", "gz", None, None, None)
    return jax.shard_map(
        on_device,
        mesh=mesh,
        in_specs=(cells, cells, cells, P(), P()),
        out_specs=(cells, P("rep", "gz"), P("rep", "gz")),
        check_vma=False,
    )
```

```python
import functools
import math

import jax
import jax.numpy as jnp
from jax import lax
from jax.experimental import pallas as pl
from jax.experimental.pallas import tpu as pltpu
from jax.sharding import PartitionSpec as P

leak_slope = 0.3
MESH = pl.DeviceIdType.MESH
BF = jnp.bfloat16
F32 = jnp.float32

CH = 128
ROW = 16
EDGE = 32
PLANE = EDGE * ROW
PAD = PLANE + 2 * ROW
PART = PLANE // 4


def remote(src, dst, ssem, rsem, dev):
    return pltpu.make_async_remote_copy(
        src_ref=src, dst_ref=dst, send_sem=ssem, recv_sem=rsem, device_id=dev, device_id_type=MESH
    )


class Halo:
    def __init__(self, rep, g, low, high, halo, relay, ss, rs):
        self.rep, self.g = rep, g
        self.low, self.high, self.halo, self.relay, self.ss, self.rs = low, high, halo, relay, ss, rs

    def up(self):
        return remote(self.high, self.halo.at[0], self.ss.at[0], self.rs.at[0], (self.rep, self.g + 1))

    def down(self):
        return remote(self.low, self.halo.at[1], self.ss.at[1], self.rs.at[1], (self.rep, self.g - 1))

    def parts(self, side):
        src, home, first = (self.high, 3, 0) if side == 0 else (self.low, 0, 4)
        copies = []
        for k in range(4):
            rows = pl.ds(k * PART, PART)
            if k == home:
                dst, sem, dev = self.halo.at[side, rows], self.rs.at[3 + k], (self.rep, 4 - side)
            else:
                dst, sem, dev = self.relay, self.rs.at[2], (self.rep, first + k)
            copies.append(remote(src.at[rows], dst, self.ss.at[2 + k], sem, dev))
        return copies

    def pass_on(self, side):
        k = self.g if side == 0 else self.g - 4
        return remote(
            self.relay,
            self.halo.at[side, pl.ds(pl.multiple_of(k * PART, PART), PART)],
            self.ss.at[6],
            self.rs.at[3 + k],
            (self.rep, 4 - side),
        )

    def landed(self, side, k):
        block = self.halo.at[side, pl.ds(k * PART, PART)]
        return remote(block, block, self.ss.at[2 + k], self.rs.at[3 + k], (self.rep, 3 + side))

    def send_high(self):
        @pl.when((self.g != 3) & (self.g != 7))
        def _():
            self.up().start()

        @pl.when(self.g == 3)
        def _():
            for copy in self.parts(0):
                copy.start()

    def send_low(self):
        @pl.when((self.g != 0) & (self.g != 4))
        def _():
            self.down().start()

        @pl.when(self.g == 4)
        def _():
            for copy in self.parts(1):
                copy.start()

    def send(self):
        @pl.when(self.g == 4)
        def _():
            for copy in self.parts(1):
                copy.start()

        self.send_high()

        @pl.when((self.g != 0) & (self.g != 4))
        def _():
            self.down().start()

    def forward(self):
        for side, inside in ((0, self.g < 3), (1, self.g > 4)):

            @pl.when(inside)
            def _():
                copy = self.pass_on(side)
                remote(self.relay, self.relay, self.ss.at[6], self.rs.at[2], (self.rep, 4 - side)).wait_recv()
                copy.start()

    def wait_low(self):
        @pl.when((self.g != 0) & (self.g != 4))
        def _():
            self.up().wait_recv()

        @pl.when(self.g == 4)
        def _():
            for k in range(4):
                self.landed(0, k).wait_recv()

    def wait_high(self):
        @pl.when((self.g != 3) & (self.g != 7))
        def _():
            self.down().wait_recv()

        @pl.when(self.g == 3)
        def _():
            for k in range(4):
                self.landed(1, k).wait_recv()

    def drain(self):
        @pl.when((self.g != 3) & (self.g != 7))
        def _():
            self.up().wait_send()

        @pl.when((self.g != 0) & (self.g != 4))
        def _():
            self.down().wait_send()

        @pl.when(self.g == 3)
        def _():
            for copy in self.parts(0):
                copy.wait_send()

        @pl.when(self.g == 4)
        def _():
            for copy in self.parts(1):
                copy.wait_send()

        for side, inside in ((0, self.g < 3), (1, self.g > 4)):

            @pl.when(inside)
            def _():
                self.pass_on(side).wait_send()


class Where:
    def __init__(self):
        self.rep, self.g = lax.axis_index("rep"), lax.axis_index("gz")
        self.core = lax.rem(self.rep, 2)
        self.x = lax.rem(lax.div(self.rep, 2), 4)
        self.zl = lax.div(self.rep, 8)
        self.y = lax.rem(self.g, 4)
        self.zh = lax.div(self.g, 4)
        self.z = self.zh * 8 + self.zl

    def other_core(self):
        return (self.rep + 1 - 2 * self.core, self.g)

    def at_x(self, d):
        x = lax.rem(self.x + d, 4)
        return x, (self.zl * 8 + x * 2 + self.core, self.g)

    def at_y(self, d):
        y = lax.rem(self.y + d, 4)
        return y, (self.rep, self.zh * 4 + y)

    def at_z(self, d):
        z = lax.rem(self.z + d, 16)
        rest = self.rep - self.zl * 8
        return z, (lax.rem(z, 8) * 8 + rest, lax.div(z, 8) * 4 + self.y)


class Reduce:
    def __init__(self, w, s, rc, t, r1, u, r2, zs, rz, ss, rs):
        self.w = w
        self.s, self.rc, self.t, self.r1, self.u = s, rc, t, r1, u
        self.r2, self.zs, self.rz, self.ss, self.rs = r2, zs, rz, ss, rs

    def core_copy(self, half):
        return remote(
            self.s.at[1 - self.w.core, half],
            self.rc.at[half],
            self.ss.at[half],
            self.rs.at[half],
            self.w.other_core(),
        )

    def first(self, half, d):
        place, dev = self.w.at_x(d) if half == 0 else self.w.at_y(d)
        k = 2 + half * 3 + d - 1
        return remote(self.t.at[half, place], self.r1.at[half, d - 1], self.ss.at[k], self.rs.at[k], dev)

    def second(self, half, d):
        place, dev = self.w.at_y(d) if half == 0 else self.w.at_x(d)
        k = 8 + half * 3 + d - 1
        return remote(self.u.at[half, place], self.r2.at[half, d - 1], self.ss.at[k], self.rs.at[k], dev)

    def chunk(self, zl, zh):
        within = lax.rem(zl, 4)
        return lax.div(within, 2) * 4 + zh * 2 + lax.rem(within, 2)

    def last(self, half):
        w = self.w
        copies = []
        for flip in (1, 0):
            zh = 1 - w.zh if flip else w.zh
            for k in (2, 1, 3, 0):
                zl = half * 4 + lax.rem(w.zl + k, 4)
                dev = (zl * 8 + w.rep - w.zl * 8, zh * 4 + w.y)
                copy = remote(
                    self.zs.at[half, self.chunk(zl, zh)],
                    self.rz.at[w.z],
                    self.ss.at[14 + half * 8 + flip * 4 + k],
                    self.rs.at[14 + w.z],
                    dev,
                )
                copies.append((flip == 1 or k > 0, copy))
        return copies

    def each_last(self, half, act):
        for always, copy in self.last(half):
            if always:
                act(copy)
            else:

                @pl.when(lax.div(self.w.zl, 4) != half)
                def _():
                    act(copy)

    def step_core(self, half):
        self.core_copy(half).wait_recv()
        core = self.w.core

        def body(i, carry):
            for j in range(4):
                own = self.s[core, half, i, j].astype(F32)
                self.t[half, i, j] = (own + self.rc[half, i, j].astype(F32)).astype(BF)
            return carry

        lax.fori_loop(0, 4, body, 0)
        for d in (2, 1, 3):
            self.first(half, d).start()

    def step_first(self, half):
        mine = self.w.x if half == 0 else self.w.y
        for d in (1, 3, 2):
            self.first(half, d).wait_recv()

        def body(i, carry):
            total = self.t[half, mine, i].astype(F32)
            for k in range(3):
                total += self.r1[half, k, i].astype(F32)
            self.u[half, i] = total.astype(BF)
            return carry

        lax.fori_loop(0, 4, body, 0)
        for d in (2, 1, 3):
            self.second(half, d).start()

    def step_second(self, half):
        mine = self.w.y if half == 0 else self.w.x
        for d in (1, 3, 2):
            self.second(half, d).wait_recv()
        total = self.u[half, mine].astype(F32)
        for k in range(3):
            total += self.r2[half, k].astype(F32)
        self.zs[half] = total.reshape(8, 8, CH)
        self.each_last(half, lambda copy: copy.start())

    def finish(self, out, factor):
        w = self.w
        total = self.zs[lax.div(w.zl, 4), self.chunk(w.zl, w.zh)]
        for d in (1, 15, 2, 14, 3, 13, 4, 12, 5, 11, 6, 10, 7, 9, 8):
            z, dev = w.at_z(d)
            remote(self.zs.at[0, 0], self.rz.at[z], self.ss.at[14], self.rs.at[14 + z], dev).wait_recv()
            total += self.rz[z]
        out[...] = total * factor

    def drain(self):
        for half in range(2):
            self.core_copy(half).wait_send()
            for d in (1, 2, 3):
                self.first(half, d).wait_send()
                self.second(half, d).wait_send()
            self.each_last(half, lambda copy: copy.wait_send())


def regroup(flat, s, half):
    group = lax.broadcasted_iota(jnp.int32, (16, CH), 1)
    masks = {b: lax.rem(lax.div(group, 16 * b), 2) == 1 for b in (1, 2, 4)}

    def body(pair, carry):
        block = flat.at[pl.ds(pl.multiple_of((half * 2 + pair) * 864, 8), 872)]
        for x in range(4):
            for core in range(2):
                base = x * 108 + core * 54
                v = []
                for q in range(8):
                    at = base + 7 * q
                    both = jnp.concatenate([block[at : at + 8, :], block[at + 432 : at + 440, :]], axis=0)
                    v.append(both.astype(BF))
                for b in (1, 2, 4):
                    for q in range(8):
                        if q & b:
                            continue
                        a, c = v[q], v[q | b]
                        v[q] = jnp.where(masks[b], pltpu.roll(c, 16 * b, 1), a)
                        v[q | b] = jnp.where(masks[b], c, pltpu.roll(a, CH - 16 * b, 1))
                for q in range(8):
                    rows = pl.ds(pl.multiple_of(pair * 32 + (q // 4) * 16, 16), 16)
                    if half == 0:
                        s[core, 0, x, q % 4, rows, :] = v[q]
                    else:
                        s[core, 1, q % 4, x, rows, :] = v[q]
        return carry

    lax.fori_loop(0, 2, body, 0)


def spread(plane, ext, at):
    wide = plane.astype(F32)
    col = lax.rem(lax.broadcasted_iota(jnp.int32, (PLANE, CH), 0), ROW)
    before = jnp.where(col == 0, 0.0, pltpu.roll(wide, 1, 0)).astype(BF)
    after = jnp.where(col == ROW - 1, 0.0, pltpu.roll(wide, PLANE - 1, 0)).astype(BF)
    rows = slice(ROW, ROW + PLANE)
    ext[at, rows, 0:CH] = before
    ext[at, rows, CH : 2 * CH] = plane
    ext[at, rows, 2 * CH : 3 * CH] = after


def slabs(ext, at):
    return jnp.concatenate([ext[at, dy * ROW : dy * ROW + PLANE, :] for dy in range(3)], axis=1)


def mm(a, b):
    return jnp.dot(a, b, preferred_element_type=F32)


def lay_weights(w, wt):
    for a in range(3):
        for dy in range(3):
            for dx in range(3):
                k = dy * 3 + dx
                wt[a, k * CH : (k + 1) * CH, :] = w[9 * a + 8 - k].T


def inner_data_grad(ext, wt, acc):
    for at in (1, 2):
        x = slabs(ext, at)
        pair = jnp.concatenate([wt[2 - at], wt[3 - at]], axis=1)
        if at == 1:
            acc[...] = mm(x, pair)
        else:
            acc[...] += mm(x, pair)


def kernel(
    factor, li_h, pa_h, ct_h, w1_h, w2_h, ig, tiles,
    li, pa, ct, w1, w2, ig_v, ct_halo, li_halo, pg_halo, ct_relay, li_relay, pg_relay,
    e_ct, e_pg, pg, act_t, li_t, wt2, wt1, acc, flat1, flat2,
    s1, rc1, t1, r11, u1, r21, zs1, rz1, s2, rc2, t2, r12, u2, r22, zs2, rz2,
    in_sem, hs_ct, hr_ct, hs_li, hr_li, hs_pg, hr_pg, ss1, rs1, ss2, rs2,
):
    w = Where()
    rep, g = w.rep, w.g
    barrier = pltpu.get_barrier_semaphore()
    peers = [w.other_core()]
    peers += [w.at_x(d)[1] for d in (1, 2, 3)] + [w.at_y(d)[1] for d in (1, 2, 3)]
    peers += [w.at_z(d)[1] for d in range(1, 16)]
    for dev in peers:
        pl.semaphore_signal(barrier, inc=1, device_id=dev, device_id_type=MESH)
    for end, senders in ((3, (4, 5, 6)), (4, (1, 2, 3))):

        @pl.when(g == end)
        def _():
            for k in senders:
                pl.semaphore_signal(barrier, inc=1, device_id=(rep, k), device_id_type=MESH)

    loads = [
        pltpu.make_async_copy(a, b, in_sem.at[k])
        for k, (a, b) in enumerate([(ct_h, ct), (w2_h, w2), (pa_h, pa), (li_h, li), (w1_h, w1)])
    ]
    for load in loads:
        load.start()

    @pl.when(g == 0)
    def _():
        for halo in (ct_halo, li_halo, pg_halo):
            halo[0] = jnp.zeros((PLANE, CH), BF)

    @pl.when(g == 7)
    def _():
        for halo in (ct_halo, li_halo, pg_halo):
            halo[1] = jnp.zeros((PLANE, CH), BF)

    edge = jnp.zeros((4, ROW, 3 * CH), BF)
    for ext in (e_ct, e_pg):
        ext[:, 0:ROW, :] = edge
        ext[:, ROW + PLANE : PAD, :] = edge
    for flat in (flat1, flat2):
        flat[27 * CH : 27 * CH + 8, :] = jnp.zeros((8, CH), F32)
    loads[0].wait()

    between = (g > 0) & (g < 7)

    @pl.when(between)
    def _():
        pl.semaphore_wait(barrier, len(peers) + 1)

    @pl.when(jnp.logical_not(between))
    def _():
        pl.semaphore_wait(barrier, len(peers))

    low, high = pl.ds(0, PLANE), pl.ds(PLANE, PLANE)
    h_ct = Halo(rep, g, ct.at[low], ct.at[high], ct_halo, ct_relay, hs_ct, hr_ct)
    h_li = Halo(rep, g, li.at[low], li.at[high], li_halo, li_relay, hs_li, hr_li)
    h_pg = Halo(rep, g, pg.at[low], pg.at[high], pg_halo, pg_relay, hs_pg, hr_pg)
    red1 = Reduce(w, s1, rc1, t1, r11, u1, r21, zs1, rz1, ss1, rs1)
    red2 = Reduce(w, s2, rc2, t2, r12, u2, r22, zs2, rz2, ss2, rs2)
    h_ct.send()
    spread(ct[low, :], e_ct, 1)
    spread(ct[high, :], e_ct, 2)
    loads[1].wait()
    lay_weights(w2, wt2)
    h_ct.forward()
    loads[3].wait()
    h_li.send()
    inner_data_grad(e_ct, wt2, acc)
    loads[2].wait()
    for q in range(2):
        v = pa[q * PLANE : (q + 1) * PLANE, :].astype(F32)
        act = jnp.where(v > 0, v, leak_slope * v).astype(BF)
        act_t[:, q * PLANE : (q + 1) * PLANE] = act.T
    li_t[:, PLANE : 2 * PLANE] = li[low, :].T
    li_t[:, 2 * PLANE : 3 * PLANE] = li[high, :].T
    h_li.forward()

    order = [(0, 1), (2, 3), (4, 5), (6, 7), (8,)]

    def taps(ext, at, group):
        parts = []
        for k in group:
            dy, dx = 2 - k // 3, 2 - k % 3
            parts.append(ext[at, dy * ROW : dy * ROW + PLANE, dx * CH : (dx + 1) * CH])
        return parts[0] if len(parts) == 1 else jnp.concatenate(parts, axis=1)

    def put(flat, group, a, value, more=False):
        for j, k in enumerate(group):
            t = 9 * a + k
            rows = slice(t * CH, (t + 1) * CH)
            tap = value[:, j * CH : (j + 1) * CH]
            flat[rows, :] = flat[rows, :] + tap if more else tap

    a0, a1 = act_t[:, 0:PLANE], act_t[:, PLANE : 2 * PLANE]
    for group in order:
        stack = jnp.concatenate([a0, a1], axis=0)
        mid = mm(stack, taps(e_ct, 1, group))
        after = mm(stack, taps(e_ct, 2, group))
        put(flat2, group, 0, after[:CH])
        put(flat2, group, 1, mid[:CH] + after[CH:])
        put(flat2, group, 2, mid[CH:])
    loads[4].wait()
    lay_weights(w1, wt1)

    for q in range(2):
        if q == 0:
            h_ct.wait_low()
        else:
            h_ct.wait_high()
        spread(ct_halo[q], e_ct, 3 * q)
        total = acc[:, q * CH : (q + 1) * CH] + mm(slabs(e_ct, 3 * q), wt2[2 - 2 * q])
        rows = pl.ds(q * PLANE, PLANE)
        v = pa[rows, :].astype(F32)
        pg[rows, :] = (total * jnp.where(v > 0, 1.0, leak_slope)).astype(BF)
        if q == 0:
            h_pg.send_low()
        else:
            h_pg.send_high()

    def edge_two():
        for group in order:
            put(flat2, group, 0, mm(a1, taps(e_ct, 3, group)), more=True)
            put(flat2, group, 2, mm(a0, taps(e_ct, 0, group)), more=True)

    def send_two():
        for half in (0, 1):
            regroup(flat2, s2, half)
            red2.core_copy(half).start()

    def spread_pg():
        spread(pg[low, :], e_pg, 1)
        spread(pg[high, :], e_pg, 2)

    def turn_li():
        h_li.wait_low()
        li_t[:, 0:PLANE] = li_halo[0].T
        h_li.wait_high()
        li_t[:, 3 * PLANE : 4 * PLANE] = li_halo[1].T

    def grad_one():
        for group in order:
            total = None
            for at in (1, 2):
                lhs = jnp.concatenate(
                    [li_t[:, (at + a - 1) * PLANE : (at + a) * PLANE] for a in range(3)], axis=0
                )
                term = mm(lhs, taps(e_pg, at, group))
                total = term if total is None else total + term
            for a in range(3):
                put(flat1, group, a, total[a * CH : (a + 1) * CH])

    def send_one():
        for half in (0, 1):
            regroup(flat1, s1, half)
            red1.core_copy(half).start()

    def inner():
        inner_data_grad(e_pg, wt1, acc)

    def pg_low():
        h_pg.wait_low()
        spread(pg_halo[0], e_pg, 0)

    def pg_high():
        h_pg.wait_high()
        spread(pg_halo[1], e_pg, 3)

    save = pltpu.make_async_copy(ig_v, ig, in_sem.at[5])

    def outer():
        for q in range(2):
            total = acc[:, q * CH : (q + 1) * CH] + mm(slabs(e_pg, 3 * q), wt1[2 - 2 * q])
            ig_v[q * PLANE : (q + 1) * PLANE, :] = total.astype(BF)
        save.start()

    edge_two()
    send_two()
    h_pg.forward()
    spread_pg()
    turn_li()
    grad_one()
    red2.step_core(0)
    red2.step_core(1)
    send_one()
    inner()
    red1.step_core(0)
    red1.step_core(1)
    red2.step_first(0)
    red2.step_first(1)
    pg_low()
    pg_high()
    outer()
    red1.step_first(0)
    red1.step_first(1)
    red2.step_second(0)
    red2.step_second(1)
    red1.step_second(0)
    red1.step_second(1)
    red2.finish(tiles.at[1], factor)
    red1.finish(tiles.at[0], factor)
    save.wait()

    for halo in (h_ct, h_li, h_pg):
        halo.drain()
    red2.drain()
    red1.drain()


def close(ig_in, tiles_in, ig, one, two, through, tiles, turned, load_sem, save_sem):
    small = pltpu.make_async_copy(tiles_in, tiles, load_sem.at[4])
    small.start()
    rows = ig_in.shape[0] // 4
    loads, saves = [], []
    for k in range(4):
        at = pl.ds(k * rows, rows)
        loads.append(pltpu.make_async_copy(ig_in.at[at], through.at[at], load_sem.at[k]))
        saves.append(pltpu.make_async_copy(through.at[at], ig.at[at], save_sem.at[k]))
        loads[k].start()
    small.wait()
    for k, out in enumerate((one, two)):
        flip = tiles[k].T
        for q in range(8):
            size = 7 if q < 7 else 5
            turned[k, :, 7 * q : 7 * q + size] = flip[16 * q : 16 * q + 16, :size]
        saves.append(pltpu.make_async_copy(turned.at[k], out, save_sem.at[4 + k]))
        saves[4 + k].start()
    for k in range(4):
        loads[k].wait()
        saves[k].start()
    for save in saves:
        save.wait()


def reduce_buffers():
    return [
        pltpu.VMEM((2, 2, 4, 4, 64, CH), BF),
        pltpu.VMEM((2, 4, 4, 64, CH), BF),
        pltpu.VMEM((2, 4, 4, 64, CH), BF),
        pltpu.VMEM((2, 3, 4, 64, CH), BF),
        pltpu.VMEM((2, 4, 64, CH), BF),
        pltpu.VMEM((2, 3, 64, CH), BF),
        pltpu.VMEM((2, 8, 8, CH), F32),
        pltpu.VMEM((16, 8, CH), F32),
    ]


def on_device(layer_input, pre_act, cotangent, w_one, w_two):
    shape = layer_input.shape
    cells = 2 * PLANE
    factor = 1.0 / math.sqrt(cells * lax.axis_size("rep") * lax.axis_size("gz"))
    flat_in = [v.reshape(cells, CH) for v in (layer_input, pre_act, cotangent)]
    any_spec = pl.BlockSpec(memory_space=pl.ANY)
    vmem_spec = pl.BlockSpec(memory_space=pltpu.VMEM)
    dma = pltpu.SemaphoreType.DMA
    field = pltpu.VMEM((cells, CH), BF)
    kern = pltpu.VMEM((27, CH, CH), BF)
    halo = pltpu.VMEM((2, PLANE, CH), BF)
    relay = pltpu.VMEM((PART, CH), BF)
    ext = pltpu.VMEM((4, PAD, 3 * CH), BF)
    turned = pltpu.VMEM((3, 9 * CH, CH), BF)
    held, tiles = pl.pallas_call(
        functools.partial(kernel, factor),
        out_shape=(
            jax.ShapeDtypeStruct((cells, CH), BF),
            jax.ShapeDtypeStruct((2, 8, CH), F32),
        ),
        in_specs=[any_spec] * 5,
        out_specs=(any_spec, vmem_spec),
        scratch_shapes=[
            field, field, field, kern, kern, field, halo, halo, halo, relay, relay, relay,
            ext, ext, field, pltpu.VMEM((CH, cells), BF), pltpu.VMEM((CH, 2 * cells), BF),
            turned, turned, pltpu.VMEM((PLANE, 2 * CH), F32), *[pltpu.VMEM((27 * CH + 8, CH), F32)] * 2,
            *reduce_buffers(), *reduce_buffers(),
            dma((6,)), *[dma((7,))] * 6, *[dma((30,))] * 4,
        ],
        compiler_params=pltpu.CompilerParams(
            collective_id=0, has_side_effects=True, vmem_limit_bytes=62 * 2**20
        ),
    )(*flat_in, w_one, w_two)
    input_grad, one, two = pl.pallas_call(
        close,
        out_shape=(
            jax.ShapeDtypeStruct((cells, CH), BF),
            jax.ShapeDtypeStruct((16, 54), F32),
            jax.ShapeDtypeStruct((16, 54), F32),
        ),
        in_specs=[any_spec, any_spec],
        out_specs=(any_spec, any_spec, any_spec),
        scratch_shapes=[
            field, pltpu.VMEM((2, 8, CH), F32), pltpu.VMEM((2, 16, 54), F32), dma((5,)), dma((6,)),
        ],
    )(held, tiles)
    return (input_grad.reshape(shape), one.T, two.T)


def solution(mesh):
    cells = P("rep", "gz", None, None, None)
    return jax.shard_map(
        on_device,
        mesh=mesh,
        in_specs=(cells, cells, cells, P(), P()),
        out_specs=(cells, P("rep", "gz"), P("rep", "gz")),
        check_vma=False,
    )
```

```python
import functools
import math

import jax
import jax.numpy as jnp
from jax import lax
from jax.experimental import pallas as pl
from jax.experimental.pallas import tpu as pltpu
from jax.sharding import PartitionSpec as P

leak_slope = 0.3
MESH = pl.DeviceIdType.MESH
BF = jnp.bfloat16
F32 = jnp.float32

CH = 128
ROW = 16
EDGE = 32
PLANE = EDGE * ROW
PAD = PLANE + 2 * ROW
PART = PLANE // 4


def remote(src, dst, ssem, rsem, dev):
    return pltpu.make_async_remote_copy(
        src_ref=src, dst_ref=dst, send_sem=ssem, recv_sem=rsem, device_id=dev, device_id_type=MESH
    )


class Halo:
    def __init__(self, rep, g, low, high, halo, relay, ss, rs):
        self.rep, self.g = rep, g
        self.low, self.high, self.halo, self.relay, self.ss, self.rs = low, high, halo, relay, ss, rs

    def up(self):
        return remote(self.high, self.halo.at[0], self.ss.at[0], self.rs.at[0], (self.rep, self.g + 1))

    def down(self):
        return remote(self.low, self.halo.at[1], self.ss.at[1], self.rs.at[1], (self.rep, self.g - 1))

    def parts(self, side):
        src, home, first = (self.high, 3, 0) if side == 0 else (self.low, 0, 4)
        copies = []
        for k in range(4):
            rows = pl.ds(k * PART, PART)
            if k == home:
                dst, sem, dev = self.halo.at[side, rows], self.rs.at[3 + k], (self.rep, 4 - side)
            else:
                dst, sem, dev = self.relay, self.rs.at[2], (self.rep, first + k)
            copies.append(remote(src.at[rows], dst, self.ss.at[2 + k], sem, dev))
        return copies

    def pass_on(self, side):
        k = self.g if side == 0 else self.g - 4
        return remote(
            self.relay,
            self.halo.at[side, pl.ds(pl.multiple_of(k * PART, PART), PART)],
            self.ss.at[6],
            self.rs.at[3 + k],
            (self.rep, 4 - side),
        )

    def landed(self, side, k):
        block = self.halo.at[side, pl.ds(k * PART, PART)]
        return remote(block, block, self.ss.at[2 + k], self.rs.at[3 + k], (self.rep, 3 + side))

    def send_high(self):
        @pl.when((self.g != 3) & (self.g != 7))
        def _():
            self.up().start()

        @pl.when(self.g == 3)
        def _():
            for copy in self.parts(0):
                copy.start()

    def send_low(self):
        @pl.when((self.g != 0) & (self.g != 4))
        def _():
            self.down().start()

        @pl.when(self.g == 4)
        def _():
            for copy in self.parts(1):
                copy.start()

    def send(self):
        @pl.when(self.g == 4)
        def _():
            for copy in self.parts(1):
                copy.start()

        self.send_high()

        @pl.when((self.g != 0) & (self.g != 4))
        def _():
            self.down().start()

    def forward(self):
        for side, inside in ((0, self.g < 3), (1, self.g > 4)):

            @pl.when(inside)
            def _():
                copy = self.pass_on(side)
                remote(self.relay, self.relay, self.ss.at[6], self.rs.at[2], (self.rep, 4 - side)).wait_recv()
                copy.start()

    def wait_low(self):
        @pl.when((self.g != 0) & (self.g != 4))
        def _():
            self.up().wait_recv()

        @pl.when(self.g == 4)
        def _():
            for k in range(4):
                self.landed(0, k).wait_recv()

    def wait_high(self):
        @pl.when((self.g != 3) & (self.g != 7))
        def _():
            self.down().wait_recv()

        @pl.when(self.g == 3)
        def _():
            for k in range(4):
                self.landed(1, k).wait_recv()

    def drain(self):
        @pl.when((self.g != 3) & (self.g != 7))
        def _():
            self.up().wait_send()

        @pl.when((self.g != 0) & (self.g != 4))
        def _():
            self.down().wait_send()

        @pl.when(self.g == 3)
        def _():
            for copy in self.parts(0):
                copy.wait_send()

        @pl.when(self.g == 4)
        def _():
            for copy in self.parts(1):
                copy.wait_send()

        for side, inside in ((0, self.g < 3), (1, self.g > 4)):

            @pl.when(inside)
            def _():
                self.pass_on(side).wait_send()


class Where:
    def __init__(self):
        self.rep, self.g = lax.axis_index("rep"), lax.axis_index("gz")
        self.core = lax.rem(self.rep, 2)
        self.x = lax.rem(lax.div(self.rep, 2), 4)
        self.zl = lax.div(self.rep, 8)
        self.y = lax.rem(self.g, 4)
        self.zh = lax.div(self.g, 4)
        self.z = self.zh * 8 + self.zl

    def other_core(self):
        return (self.rep + 1 - 2 * self.core, self.g)

    def at_x(self, d):
        x = lax.rem(self.x + d, 4)
        return x, (self.zl * 8 + x * 2 + self.core, self.g)

    def at_y(self, d):
        y = lax.rem(self.y + d, 4)
        return y, (self.rep, self.zh * 4 + y)

    def at_z(self, d):
        z = lax.rem(self.z + d, 16)
        rest = self.rep - self.zl * 8
        return z, (lax.rem(z, 8) * 8 + rest, lax.div(z, 8) * 4 + self.y)


class Reduce:
    def __init__(self, w, s, rc, t, r1, u, r2, zs, rz, ss, rs):
        self.w = w
        self.s, self.rc, self.t, self.r1, self.u = s, rc, t, r1, u
        self.r2, self.zs, self.rz, self.ss, self.rs = r2, zs, rz, ss, rs

    def core_copy(self, half):
        return remote(
            self.s.at[1 - self.w.core, half],
            self.rc.at[half],
            self.ss.at[half],
            self.rs.at[half],
            self.w.other_core(),
        )

    def first(self, half, d):
        place, dev = self.w.at_x(d) if half == 0 else self.w.at_y(d)
        k = 2 + half * 3 + d - 1
        return remote(self.t.at[half, place], self.r1.at[half, d - 1], self.ss.at[k], self.rs.at[k], dev)

    def second(self, half, d):
        place, dev = self.w.at_y(d) if half == 0 else self.w.at_x(d)
        k = 8 + half * 3 + d - 1
        return remote(self.u.at[half, place], self.r2.at[half, d - 1], self.ss.at[k], self.rs.at[k], dev)

    def chunk(self, zl, zh):
        within = lax.rem(zl, 4)
        return lax.div(within, 2) * 4 + zh * 2 + lax.rem(within, 2)

    def last(self, half):
        w = self.w
        copies = []
        for flip in (1, 0):
            zh = 1 - w.zh if flip else w.zh
            for k in (2, 1, 3, 0):
                zl = half * 4 + lax.rem(w.zl + k, 4)
                dev = (zl * 8 + w.rep - w.zl * 8, zh * 4 + w.y)
                copy = remote(
                    self.zs.at[half, self.chunk(zl, zh)],
                    self.rz.at[w.z],
                    self.ss.at[14 + half * 8 + flip * 4 + k],
                    self.rs.at[14 + w.z],
                    dev,
                )
                copies.append((flip == 1 or k > 0, copy))
        return copies

    def each_last(self, half, act):
        for always, copy in self.last(half):
            if always:
                act(copy)
            else:

                @pl.when(lax.div(self.w.zl, 4) != half)
                def _():
                    act(copy)

    def step_core(self, half):
        self.core_copy(half).wait_recv()
        core = self.w.core

        def body(i, carry):
            for j in range(4):
                own = self.s[core, half, i, j].astype(F32)
                self.t[half, i, j] = (own + self.rc[half, i, j].astype(F32)).astype(BF)
            return carry

        lax.fori_loop(0, 4, body, 0)
        for d in (2, 1, 3):
            self.first(half, d).start()

    def step_first(self, half):
        mine = self.w.x if half == 0 else self.w.y
        for d in (1, 3, 2):
            self.first(half, d).wait_recv()

        def body(i, carry):
            total = self.t[half, mine, i].astype(F32)
            for k in range(3):
                total += self.r1[half, k, i].astype(F32)
            self.u[half, i] = total.astype(BF)
            return carry

        lax.fori_loop(0, 4, body, 0)
        for d in (2, 1, 3):
            self.second(half, d).start()

    def step_second(self, half):
        mine = self.w.y if half == 0 else self.w.x
        for d in (1, 3, 2):
            self.second(half, d).wait_recv()
        total = self.u[half, mine].astype(F32)
        for k in range(3):
            total += self.r2[half, k].astype(F32)
        self.zs[half] = total.reshape(8, 8, CH)
        self.each_last(half, lambda copy: copy.start())

    def finish(self, out, factor):
        w = self.w
        total = self.zs[lax.div(w.zl, 4), self.chunk(w.zl, w.zh)]
        for d in (1, 15, 2, 14, 3, 13, 4, 12, 5, 11, 6, 10, 7, 9, 8):
            z, dev = w.at_z(d)
            remote(self.zs.at[0, 0], self.rz.at[z], self.ss.at[14], self.rs.at[14 + z], dev).wait_recv()
            total += self.rz[z]
        out[...] = total * factor

    def drain(self):
        for half in range(2):
            self.core_copy(half).wait_send()
            for d in (1, 2, 3):
                self.first(half, d).wait_send()
                self.second(half, d).wait_send()
            self.each_last(half, lambda copy: copy.wait_send())


def regroup(flat, s, half):
    group = lax.broadcasted_iota(jnp.int32, (16, CH), 1)
    masks = {b: lax.rem(lax.div(group, 16 * b), 2) == 1 for b in (1, 2, 4)}

    def body(pair, carry):
        block = flat.at[pl.ds(pl.multiple_of((half * 2 + pair) * 864, 8), 872)]
        for x in range(4):
            for core in range(2):
                base = x * 108 + core * 54
                v = []
                for q in range(8):
                    at = base + 7 * q
                    both = jnp.concatenate([block[at : at + 8, :], block[at + 432 : at + 440, :]], axis=0)
                    v.append(both.astype(BF))
                for b in (1, 2, 4):
                    for q in range(8):
                        if q & b:
                            continue
                        a, c = v[q], v[q | b]
                        v[q] = jnp.where(masks[b], pltpu.roll(c, 16 * b, 1), a)
                        v[q | b] = jnp.where(masks[b], c, pltpu.roll(a, CH - 16 * b, 1))
                for q in range(8):
                    rows = pl.ds(pl.multiple_of(pair * 32 + (q // 4) * 16, 16), 16)
                    if half == 0:
                        s[core, 0, x, q % 4, rows, :] = v[q]
                    else:
                        s[core, 1, q % 4, x, rows, :] = v[q]
        return carry

    lax.fori_loop(0, 2, body, 0)


def spread(plane, ext, at):
    wide = plane.astype(F32)
    col = lax.rem(lax.broadcasted_iota(jnp.int32, (PLANE, CH), 0), ROW)
    before = jnp.where(col == 0, 0.0, pltpu.roll(wide, 1, 0)).astype(BF)
    after = jnp.where(col == ROW - 1, 0.0, pltpu.roll(wide, PLANE - 1, 0)).astype(BF)
    rows = slice(ROW, ROW + PLANE)
    ext[at, rows, 0:CH] = before
    ext[at, rows, CH : 2 * CH] = plane
    ext[at, rows, 2 * CH : 3 * CH] = after


def slabs(ext, at):
    return jnp.concatenate([ext[at, dy * ROW : dy * ROW + PLANE, :] for dy in range(3)], axis=1)


def mm(a, b):
    return jnp.dot(a, b, preferred_element_type=F32)


def lay_weights(w, wt):
    for a in range(3):
        for dy in range(3):
            for dx in range(3):
                k = dy * 3 + dx
                wt[a, k * CH : (k + 1) * CH, :] = w[9 * a + 8 - k].T


def inner_data_grad(ext, wt, acc):
    for at in (1, 2):
        x = slabs(ext, at)
        pair = jnp.concatenate([wt[2 - at], wt[3 - at]], axis=1)
        both = mm(x, pair)
        for q in range(2):
            part = both[:, q * CH : (q + 1) * CH]
            acc[q] = part if at == 1 else acc[q] + part


def kernel(
    factor, li_h, pa_h, ct_h, w1_h, w2_h, ig, tiles,
    li, pa, ct, w1, w2, ig_v, ct_halo, li_halo, pg_halo, ct_relay, li_relay, pg_relay,
    e_ct, e_pg, pg, act_t, li_t, wt2, wt1, acc, flat1, flat2,
    s1, rc1, t1, r11, u1, r21, zs1, rz1, s2, rc2, t2, r12, u2, r22, zs2, rz2,
    in_sem, hs_ct, hr_ct, hs_li, hr_li, hs_pg, hr_pg, ss1, rs1, ss2, rs2,
):
    w = Where()
    rep, g = w.rep, w.g
    barrier = pltpu.get_barrier_semaphore()
    peers = [w.other_core()]
    peers += [w.at_x(d)[1] for d in (1, 2, 3)] + [w.at_y(d)[1] for d in (1, 2, 3)]
    far_first = (8, 7, 9, 6, 10, 5, 11, 4, 12, 3, 13, 2, 14, 1, 15)
    peers = [w.at_z(d)[1] for d in far_first] + peers
    for dev in peers:
        pl.semaphore_signal(barrier, inc=1, device_id=dev, device_id_type=MESH)
    for end, senders in ((3, (4, 5, 6)), (4, (1, 2, 3))):

        @pl.when(g == end)
        def _():
            for k in senders:
                pl.semaphore_signal(barrier, inc=1, device_id=(rep, k), device_id_type=MESH)

    loads = [
        pltpu.make_async_copy(a, b, in_sem.at[k])
        for k, (a, b) in enumerate([(ct_h, ct), (w2_h, w2), (pa_h, pa), (li_h, li), (w1_h, w1)])
    ]
    for load in loads:
        load.start()

    @pl.when(g == 0)
    def _():
        for halo in (ct_halo, li_halo, pg_halo):
            halo[0] = jnp.zeros((PLANE, CH), BF)

    @pl.when(g == 7)
    def _():
        for halo in (ct_halo, li_halo, pg_halo):
            halo[1] = jnp.zeros((PLANE, CH), BF)

    edge = jnp.zeros((4, ROW, 3 * CH), BF)
    for ext in (e_ct, e_pg):
        ext[:, 0:ROW, :] = edge
        ext[:, ROW + PLANE : PAD, :] = edge
    for flat in (flat1, flat2):
        flat[27 * CH : 27 * CH + 8, :] = jnp.zeros((8, CH), F32)
    loads[0].wait()

    between = (g > 0) & (g < 7)

    @pl.when(between)
    def _():
        pl.semaphore_wait(barrier, len(peers) + 1)

    @pl.when(jnp.logical_not(between))
    def _():
        pl.semaphore_wait(barrier, len(peers))

    low, high = pl.ds(0, PLANE), pl.ds(PLANE, PLANE)
    h_ct = Halo(rep, g, ct.at[low], ct.at[high], ct_halo, ct_relay, hs_ct, hr_ct)
    h_li = Halo(rep, g, li.at[low], li.at[high], li_halo, li_relay, hs_li, hr_li)
    h_pg = Halo(rep, g, pg.at[low], pg.at[high], pg_halo, pg_relay, hs_pg, hr_pg)
    red1 = Reduce(w, s1, rc1, t1, r11, u1, r21, zs1, rz1, ss1, rs1)
    red2 = Reduce(w, s2, rc2, t2, r12, u2, r22, zs2, rz2, ss2, rs2)
    h_ct.send()
    spread(ct[low, :], e_ct, 1)
    spread(ct[high, :], e_ct, 2)
    loads[1].wait()
    lay_weights(w2, wt2)
    h_ct.forward()
    loads[3].wait()
    h_li.send()
    inner_data_grad(e_ct, wt2, acc)
    loads[2].wait()
    for q in range(2):
        v = pa[q * PLANE : (q + 1) * PLANE, :].astype(F32)
        act = jnp.where(v > 0, v, leak_slope * v).astype(BF)
        act_t[q] = act.T
    li_t[1] = li[low, :].T
    li_t[2] = li[high, :].T
    h_li.forward()

    order = [(0, 1), (2, 3), (4, 5), (6, 7), (8,)]

    def taps(ext, at, group):
        parts = []
        for k in group:
            dy, dx = 2 - k // 3, 2 - k % 3
            parts.append(ext[at, dy * ROW : dy * ROW + PLANE, dx * CH : (dx + 1) * CH])
        return parts[0] if len(parts) == 1 else jnp.concatenate(parts, axis=1)

    def put(flat, group, a, value, more=False):
        for j, k in enumerate(group):
            t = 9 * a + k
            rows = pl.ds(pl.multiple_of(t * CH, CH), CH)
            tap = value[:, j * CH : (j + 1) * CH]
            flat[rows, :] = flat[rows, :] + tap if more else tap

    for group in order:
        stack = jnp.concatenate([act_t[0], act_t[1]], axis=0)
        mid = mm(stack, taps(e_ct, 1, group))
        after = mm(stack, taps(e_ct, 2, group))
        put(flat2, group, 0, after[:CH])
        put(flat2, group, 1, mid[:CH] + after[CH:])
        put(flat2, group, 2, mid[CH:])
    loads[4].wait()
    lay_weights(w1, wt1)

    near = lax.div(g, 4)

    def pre_grad(q):
        @pl.when(q == 0)
        def _():
            h_ct.wait_low()

        @pl.when(q == 1)
        def _():
            h_ct.wait_high()

        spread(ct_halo[q], e_ct, 3 * q)
        total = acc[q] + mm(slabs(e_ct, 3 * q), wt2[2 - 2 * q])
        rows = pl.ds(pl.multiple_of(q * PLANE, PLANE), PLANE)
        v = pa[rows, :].astype(F32)
        own = (total * jnp.where(v > 0, 1.0, leak_slope)).astype(BF)
        pg[rows, :] = own
        spread(own, e_pg, 1 + q)

        @pl.when(q == 0)
        def _():
            h_pg.send_low()

        @pl.when(q == 1)
        def _():
            h_pg.send_high()

    def edge_two(q):
        for group in order:
            put(flat2, group, 2 - 2 * q, mm(act_t[q], taps(e_ct, 3 * q, group)), more=True)

    def turn_li(q):
        @pl.when(q == 0)
        def _():
            h_li.wait_low()

        @pl.when(q == 1)
        def _():
            h_li.wait_high()

        li_t[3 * q] = li_halo[q].T

    def grad_one(q, more):
        for group in order:
            lhs = jnp.concatenate([li_t[q + a] for a in range(3)], axis=0)
            total = mm(lhs, taps(e_pg, 1 + q, group))
            for a in range(3):
                put(flat1, group, a, total[a * CH : (a + 1) * CH], more)

    def send(flat, s, red):
        for half in (0, 1):
            regroup(flat, s, half)
            red.core_copy(half).start()

    def inner():
        inner_data_grad(e_pg, wt1, acc)

    def pg_low():
        h_pg.wait_low()
        spread(pg_halo[0], e_pg, 0)

    def pg_high():
        h_pg.wait_high()
        spread(pg_halo[1], e_pg, 3)

    save = pltpu.make_async_copy(ig_v, ig, in_sem.at[5])

    def outer():
        for q in range(2):
            total = acc[q] + mm(slabs(e_pg, 3 * q), wt1[2 - 2 * q])
            ig_v[q * PLANE : (q + 1) * PLANE, :] = total.astype(BF)
        save.start()

    pre_grad(near)
    edge_two(near)
    turn_li(near)
    grad_one(near, False)
    pre_grad(1 - near)
    edge_two(1 - near)
    send(flat2, s2, red2)
    h_pg.forward()
    turn_li(1 - near)
    grad_one(1 - near, True)
    red2.step_core(0)
    red2.step_core(1)
    send(flat1, s1, red1)
    inner()
    red1.step_core(0)
    red1.step_core(1)
    red2.step_first(0)
    red2.step_first(1)
    pg_low()
    pg_high()
    outer()
    red1.step_first(0)
    red1.step_first(1)
    red2.step_second(0)
    red2.step_second(1)
    red1.step_second(0)
    red1.step_second(1)
    red2.finish(tiles.at[1], factor)
    red1.finish(tiles.at[0], factor)
    save.wait()

    for halo in (h_ct, h_li, h_pg):
        halo.drain()
    red2.drain()
    red1.drain()


def close(ig_in, tiles_in, ig, one, two, through, tiles, turned, load_sem, save_sem):
    small = pltpu.make_async_copy(tiles_in, tiles, load_sem.at[4])
    small.start()
    rows = ig_in.shape[0] // 4
    loads, saves = [], []
    for k in range(4):
        at = pl.ds(k * rows, rows)
        loads.append(pltpu.make_async_copy(ig_in.at[at], through.at[at], load_sem.at[k]))
        saves.append(pltpu.make_async_copy(through.at[at], ig.at[at], save_sem.at[k]))
        loads[k].start()
    small.wait()
    for k, out in enumerate((one, two)):
        flip = tiles[k].T
        for q in range(8):
            size = 7 if q < 7 else 5
            turned[k, :, 7 * q : 7 * q + size] = flip[16 * q : 16 * q + 16, :size]
        saves.append(pltpu.make_async_copy(turned.at[k], out, save_sem.at[4 + k]))
        saves[4 + k].start()
    for k in range(4):
        loads[k].wait()
        saves[k].start()
    for save in saves:
        save.wait()


def reduce_buffers():
    return [
        pltpu.VMEM((2, 2, 4, 4, 64, CH), BF),
        pltpu.VMEM((2, 4, 4, 64, CH), BF),
        pltpu.VMEM((2, 4, 4, 64, CH), BF),
        pltpu.VMEM((2, 3, 4, 64, CH), BF),
        pltpu.VMEM((2, 4, 64, CH), BF),
        pltpu.VMEM((2, 3, 64, CH), BF),
        pltpu.VMEM((2, 8, 8, CH), F32),
        pltpu.VMEM((16, 8, CH), F32),
    ]


def on_device(layer_input, pre_act, cotangent, w_one, w_two):
    shape = layer_input.shape
    cells = 2 * PLANE
    factor = 1.0 / math.sqrt(cells * lax.axis_size("rep") * lax.axis_size("gz"))
    flat_in = [v.reshape(cells, CH) for v in (layer_input, pre_act, cotangent)]
    any_spec = pl.BlockSpec(memory_space=pl.ANY)
    vmem_spec = pl.BlockSpec(memory_space=pltpu.VMEM)
    dma = pltpu.SemaphoreType.DMA
    field = pltpu.VMEM((cells, CH), BF)
    kern = pltpu.VMEM((27, CH, CH), BF)
    halo = pltpu.VMEM((2, PLANE, CH), BF)
    relay = pltpu.VMEM((PART, CH), BF)
    ext = pltpu.VMEM((4, PAD, 3 * CH), BF)
    turned = pltpu.VMEM((3, 9 * CH, CH), BF)
    held, tiles = pl.pallas_call(
        functools.partial(kernel, factor),
        out_shape=(
            jax.ShapeDtypeStruct((cells, CH), BF),
            jax.ShapeDtypeStruct((2, 8, CH), F32),
        ),
        in_specs=[any_spec] * 5,
        out_specs=(any_spec, vmem_spec),
        scratch_shapes=[
            field, field, field, kern, kern, field, halo, halo, halo, relay, relay, relay,
            ext, ext, field, pltpu.VMEM((2, CH, PLANE), BF), pltpu.VMEM((4, CH, PLANE), BF),
            turned, turned, pltpu.VMEM((2, PLANE, CH), F32), *[pltpu.VMEM((27 * CH + 8, CH), F32)] * 2,
            *reduce_buffers(), *reduce_buffers(),
            dma((6,)), *[dma((7,))] * 6, *[dma((30,))] * 4,
        ],
        compiler_params=pltpu.CompilerParams(
            collective_id=0, has_side_effects=True, vmem_limit_bytes=62 * 2**20
        ),
    )(*flat_in, w_one, w_two)
    input_grad, one, two = pl.pallas_call(
        close,
        out_shape=(
            jax.ShapeDtypeStruct((cells, CH), BF),
            jax.ShapeDtypeStruct((16, 54), F32),
            jax.ShapeDtypeStruct((16, 54), F32),
        ),
        in_specs=[any_spec, any_spec],
        out_specs=(any_spec, any_spec, any_spec),
        scratch_shapes=[
            field, pltpu.VMEM((2, 8, CH), F32), pltpu.VMEM((2, 16, 54), F32), dma((5,)), dma((6,)),
        ],
    )(held, tiles)
    return (input_grad.reshape(shape), one.T, two.T)


def solution(mesh):
    cells = P("rep", "gz", None, None, None)
    return jax.shard_map(
        on_device,
        mesh=mesh,
        in_specs=(cells, cells, cells, P(), P()),
        out_specs=(cells, P("rep", "gz"), P("rep", "gz")),
        check_vma=False,
    )
```

```python
import functools
import math

import jax
import jax.numpy as jnp
from jax import lax
from jax.experimental import pallas as pl
from jax.experimental.pallas import tpu as pltpu
from jax.sharding import PartitionSpec as P

leak_slope = 0.3
MESH = pl.DeviceIdType.MESH
BF = jnp.bfloat16
F32 = jnp.float32

CH = 128
ROW = 16
EDGE = 32
PLANE = EDGE * ROW
PAD = PLANE + 2 * ROW
PART = PLANE // 4


def remote(src, dst, ssem, rsem, dev):
    return pltpu.make_async_remote_copy(
        src_ref=src, dst_ref=dst, send_sem=ssem, recv_sem=rsem, device_id=dev, device_id_type=MESH
    )


class Halo:
    def __init__(self, rep, g, low, high, halo, relay, ss, rs):
        self.rep, self.g = rep, g
        self.low, self.high, self.halo, self.relay, self.ss, self.rs = low, high, halo, relay, ss, rs

    def up(self):
        return remote(self.high, self.halo.at[0], self.ss.at[0], self.rs.at[0], (self.rep, self.g + 1))

    def down(self):
        return remote(self.low, self.halo.at[1], self.ss.at[1], self.rs.at[1], (self.rep, self.g - 1))

    def parts(self, side):
        src, home, first = (self.high, 3, 0) if side == 0 else (self.low, 0, 4)
        copies = []
        for k in range(4):
            rows = pl.ds(k * PART, PART)
            if k == home:
                dst, sem, dev = self.halo.at[side, rows], self.rs.at[3 + k], (self.rep, 4 - side)
            else:
                dst, sem, dev = self.relay, self.rs.at[2], (self.rep, first + k)
            copies.append(remote(src.at[rows], dst, self.ss.at[2 + k], sem, dev))
        return copies

    def pass_on(self, side):
        k = self.g if side == 0 else self.g - 4
        return remote(
            self.relay,
            self.halo.at[side, pl.ds(pl.multiple_of(k * PART, PART), PART)],
            self.ss.at[6],
            self.rs.at[3 + k],
            (self.rep, 4 - side),
        )

    def landed(self, side, k):
        block = self.halo.at[side, pl.ds(k * PART, PART)]
        return remote(block, block, self.ss.at[2 + k], self.rs.at[3 + k], (self.rep, 3 + side))

    def send_high(self):
        @pl.when((self.g != 3) & (self.g != 7))
        def _():
            self.up().start()

        @pl.when(self.g == 3)
        def _():
            for copy in self.parts(0):
                copy.start()

    def send_low(self):
        @pl.when((self.g != 0) & (self.g != 4))
        def _():
            self.down().start()

        @pl.when(self.g == 4)
        def _():
            for copy in self.parts(1):
                copy.start()

    def send(self):
        @pl.when(self.g == 4)
        def _():
            for copy in self.parts(1):
                copy.start()

        self.send_high()

        @pl.when((self.g != 0) & (self.g != 4))
        def _():
            self.down().start()

    def forward(self):
        for side, inside in ((0, self.g < 3), (1, self.g > 4)):

            @pl.when(inside)
            def _():
                copy = self.pass_on(side)
                remote(self.relay, self.relay, self.ss.at[6], self.rs.at[2], (self.rep, 4 - side)).wait_recv()
                copy.start()

    def wait_low(self):
        @pl.when((self.g != 0) & (self.g != 4))
        def _():
            self.up().wait_recv()

        @pl.when(self.g == 4)
        def _():
            for k in range(4):
                self.landed(0, k).wait_recv()

    def wait_high(self):
        @pl.when((self.g != 3) & (self.g != 7))
        def _():
            self.down().wait_recv()

        @pl.when(self.g == 3)
        def _():
            for k in range(4):
                self.landed(1, k).wait_recv()

    def drain(self):
        @pl.when((self.g != 3) & (self.g != 7))
        def _():
            self.up().wait_send()

        @pl.when((self.g != 0) & (self.g != 4))
        def _():
            self.down().wait_send()

        @pl.when(self.g == 3)
        def _():
            for copy in self.parts(0):
                copy.wait_send()

        @pl.when(self.g == 4)
        def _():
            for copy in self.parts(1):
                copy.wait_send()

        for side, inside in ((0, self.g < 3), (1, self.g > 4)):

            @pl.when(inside)
            def _():
                self.pass_on(side).wait_send()


class Where:
    def __init__(self):
        self.rep, self.g = lax.axis_index("rep"), lax.axis_index("gz")
        self.core = lax.rem(self.rep, 2)
        self.x = lax.rem(lax.div(self.rep, 2), 4)
        self.zl = lax.div(self.rep, 8)
        self.y = lax.rem(self.g, 4)
        self.zh = lax.div(self.g, 4)
        self.z = self.zh * 8 + self.zl

    def other_core(self):
        return (self.rep + 1 - 2 * self.core, self.g)

    def at_x(self, d):
        x = lax.rem(self.x + d, 4)
        return x, (self.zl * 8 + x * 2 + self.core, self.g)

    def at_y(self, d):
        y = lax.rem(self.y + d, 4)
        return y, (self.rep, self.zh * 4 + y)

    def at_z(self, d):
        z = lax.rem(self.z + d, 16)
        rest = self.rep - self.zl * 8
        return z, (lax.rem(z, 8) * 8 + rest, lax.div(z, 8) * 4 + self.y)


class Reduce:
    def __init__(self, w, s, rc, t, r1, u, r2, zs, rz, ss, rs):
        self.w = w
        self.s, self.rc, self.t, self.r1, self.u = s, rc, t, r1, u
        self.r2, self.zs, self.rz, self.ss, self.rs = r2, zs, rz, ss, rs

    def core_copy(self, half):
        return remote(
            self.s.at[1 - self.w.core, half],
            self.rc.at[half],
            self.ss.at[half],
            self.rs.at[half],
            self.w.other_core(),
        )

    def first(self, half, d):
        place, dev = self.w.at_x(d) if half == 0 else self.w.at_y(d)
        k = 2 + half * 3 + d - 1
        return remote(self.t.at[half, place], self.r1.at[half, d - 1], self.ss.at[k], self.rs.at[k], dev)

    def second(self, half, d):
        place, dev = self.w.at_y(d) if half == 0 else self.w.at_x(d)
        k = 8 + half * 3 + d - 1
        return remote(self.u.at[half, place], self.r2.at[half, d - 1], self.ss.at[k], self.rs.at[k], dev)

    def chunk(self, zl, zh):
        within = lax.rem(zl, 4)
        return lax.div(within, 2) * 4 + zh * 2 + lax.rem(within, 2)

    def last(self, half):
        w = self.w
        copies = []
        for flip in (1, 0):
            zh = 1 - w.zh if flip else w.zh
            for k in (2, 1, 3, 0):
                zl = half * 4 + lax.rem(w.zl + k, 4)
                dev = (zl * 8 + w.rep - w.zl * 8, zh * 4 + w.y)
                copy = remote(
                    self.zs.at[half, self.chunk(zl, zh)],
                    self.rz.at[w.z],
                    self.ss.at[14 + half * 8 + flip * 4 + k],
                    self.rs.at[14 + w.z],
                    dev,
                )
                copies.append((flip == 1 or k > 0, copy))
        return copies

    def each_last(self, half, act):
        for always, copy in self.last(half):
            if always:
                act(copy)
            else:

                @pl.when(lax.div(self.w.zl, 4) != half)
                def _():
                    act(copy)

    def step_core(self, half):
        self.core_copy(half).wait_recv()
        core = self.w.core

        def body(i, carry):
            for j in range(4):
                own = self.s[core, half, i, j].astype(F32)
                self.t[half, i, j] = (own + self.rc[half, i, j].astype(F32)).astype(BF)
            return carry

        lax.fori_loop(0, 4, body, 0)
        for d in (2, 1, 3):
            self.first(half, d).start()

    def step_first(self, half):
        mine = self.w.x if half == 0 else self.w.y
        for d in (1, 3, 2):
            self.first(half, d).wait_recv()

        def body(i, carry):
            total = self.t[half, mine, i].astype(F32)
            for k in range(3):
                total += self.r1[half, k, i].astype(F32)
            self.u[half, i] = total.astype(BF)
            return carry

        lax.fori_loop(0, 4, body, 0)
        for d in (2, 1, 3):
            self.second(half, d).start()

    def step_second(self, half):
        mine = self.w.y if half == 0 else self.w.x
        for d in (1, 3, 2):
            self.second(half, d).wait_recv()
        total = self.u[half, mine].astype(F32)
        for k in range(3):
            total += self.r2[half, k].astype(F32)
        self.zs[half] = total.reshape(8, 8, CH)
        self.each_last(half, lambda copy: copy.start())

    def finish(self, out, factor):
        w = self.w
        total = self.zs[lax.div(w.zl, 4), self.chunk(w.zl, w.zh)]
        for d in (1, 15, 2, 14, 3, 13, 4, 12, 5, 11, 6, 10, 7, 9, 8):
            z, dev = w.at_z(d)
            remote(self.zs.at[0, 0], self.rz.at[z], self.ss.at[14], self.rs.at[14 + z], dev).wait_recv()
            total += self.rz[z]
        out[...] = total * factor

    def drain(self):
        for half in range(2):
            self.core_copy(half).wait_send()
            for d in (1, 2, 3):
                self.first(half, d).wait_send()
                self.second(half, d).wait_send()
            self.each_last(half, lambda copy: copy.wait_send())


def regroup(flat, s, red):
    group = lax.broadcasted_iota(jnp.int32, (16, CH), 1)
    masks = {b: lax.rem(lax.div(group, 16 * b), 2) == 1 for b in (1, 2, 4)}

    def body(step, carry):
        half, pair = lax.div(step, 2), lax.rem(step, 2)
        block = flat.at[pl.ds(pl.multiple_of(step * 864, 8), 872)]
        for x in range(4):
            for core in range(2):
                base = x * 108 + core * 54
                v = []
                for q in range(8):
                    at = base + 7 * q
                    both = jnp.concatenate([block[at : at + 8, :], block[at + 432 : at + 440, :]], axis=0)
                    v.append(both.astype(BF))
                for b in (1, 2, 4):
                    for q in range(8):
                        if q & b:
                            continue
                        a, c = v[q], v[q | b]
                        v[q] = jnp.where(masks[b], pltpu.roll(c, 16 * b, 1), a)
                        v[q | b] = jnp.where(masks[b], c, pltpu.roll(a, CH - 16 * b, 1))
                for q in range(8):
                    rows = pl.ds(pl.multiple_of(pair * 32 + (q // 4) * 16, 16), 16)
                    y = q % 4
                    s[core, half, x + half * (y - x), y + half * (x - y), rows, :] = v[q]

        @pl.when(pair == 1)
        def _():
            red.core_copy(half).start()

        return carry

    lax.fori_loop(0, 4, body, 0)


def spread(plane, ext, at):
    wide = plane.astype(F32)
    col = lax.rem(lax.broadcasted_iota(jnp.int32, (PLANE, CH), 0), ROW)
    before = jnp.where(col == 0, 0.0, pltpu.roll(wide, 1, 0)).astype(BF)
    after = jnp.where(col == ROW - 1, 0.0, pltpu.roll(wide, PLANE - 1, 0)).astype(BF)
    rows = slice(ROW, ROW + PLANE)
    ext[at, rows, 0:CH] = before
    ext[at, rows, CH : 2 * CH] = plane
    ext[at, rows, 2 * CH : 3 * CH] = after


def slabs(ext, at):
    return jnp.concatenate([ext[at, dy * ROW : dy * ROW + PLANE, :] for dy in range(3)], axis=1)


def mm(a, b):
    return jnp.dot(a, b, preferred_element_type=F32)


def lay_weights(w, wt):
    def body(a, carry):
        for k in range(9):
            wt[a, k * CH : (k + 1) * CH, :] = w[9 * a + 8 - k].T
        return carry

    lax.fori_loop(0, 3, body, 0)


def inner_data_grad(ext, wt, acc):
    for at in (1, 2):
        x = slabs(ext, at)
        pair = jnp.concatenate([wt[2 - at], wt[3 - at]], axis=1)
        both = mm(x, pair)
        for q in range(2):
            part = both[:, q * CH : (q + 1) * CH]
            acc[q] = part if at == 1 else acc[q] + part


def kernel(
    factor, li_h, pa_h, ct_h, w1_h, w2_h, ig, tiles,
    li, pa, ct, w1, w2, ig_v, ct_halo, li_halo, pg_halo, ct_relay, li_relay, pg_relay,
    e_ct, e_pg, pg, act_t, li_t, wt2, wt1, acc, flat1, flat2,
    s1, rc1, t1, r11, u1, r21, zs1, rz1, s2, rc2, t2, r12, u2, r22, zs2, rz2,
    in_sem, hs_ct, hr_ct, hs_li, hr_li, hs_pg, hr_pg, ss1, rs1, ss2, rs2,
):
    w = Where()
    rep, g = w.rep, w.g
    barrier = pltpu.get_barrier_semaphore()
    peers = [w.other_core()]
    peers += [w.at_x(d)[1] for d in (1, 2, 3)] + [w.at_y(d)[1] for d in (1, 2, 3)]
    far_first = (8, 7, 9, 6, 10, 5, 11, 4, 12, 3, 13, 2, 14, 1, 15)
    peers = [w.at_z(d)[1] for d in far_first] + peers
    for dev in peers:
        pl.semaphore_signal(barrier, inc=1, device_id=dev, device_id_type=MESH)
    for end, senders in ((3, (4, 5, 6)), (4, (1, 2, 3))):

        @pl.when(g == end)
        def _():
            for k in senders:
                pl.semaphore_signal(barrier, inc=1, device_id=(rep, k), device_id_type=MESH)

    loads = [
        pltpu.make_async_copy(a, b, in_sem.at[k])
        for k, (a, b) in enumerate([(ct_h, ct), (w2_h, w2), (pa_h, pa), (li_h, li), (w1_h, w1)])
    ]
    for load in loads:
        load.start()

    @pl.when(g == 0)
    def _():
        for halo in (ct_halo, li_halo, pg_halo):
            halo[0] = jnp.zeros((PLANE, CH), BF)

    @pl.when(g == 7)
    def _():
        for halo in (ct_halo, li_halo, pg_halo):
            halo[1] = jnp.zeros((PLANE, CH), BF)

    edge = jnp.zeros((4, ROW, 3 * CH), BF)
    for ext in (e_ct, e_pg):
        ext[:, 0:ROW, :] = edge
        ext[:, ROW + PLANE : PAD, :] = edge
    for flat in (flat1, flat2):
        flat[27 * CH : 27 * CH + 8, :] = jnp.zeros((8, CH), F32)
    loads[0].wait()

    between = (g > 0) & (g < 7)

    @pl.when(between)
    def _():
        pl.semaphore_wait(barrier, len(peers) + 1)

    @pl.when(jnp.logical_not(between))
    def _():
        pl.semaphore_wait(barrier, len(peers))

    low, high = pl.ds(0, PLANE), pl.ds(PLANE, PLANE)
    h_ct = Halo(rep, g, ct.at[low], ct.at[high], ct_halo, ct_relay, hs_ct, hr_ct)
    h_li = Halo(rep, g, li.at[low], li.at[high], li_halo, li_relay, hs_li, hr_li)
    h_pg = Halo(rep, g, pg.at[low], pg.at[high], pg_halo, pg_relay, hs_pg, hr_pg)
    red1 = Reduce(w, s1, rc1, t1, r11, u1, r21, zs1, rz1, ss1, rs1)
    red2 = Reduce(w, s2, rc2, t2, r12, u2, r22, zs2, rz2, ss2, rs2)
    h_ct.send()
    spread(ct[low, :], e_ct, 1)
    spread(ct[high, :], e_ct, 2)
    loads[1].wait()
    lay_weights(w2, wt2)
    h_ct.forward()
    loads[3].wait()
    h_li.send()
    inner_data_grad(e_ct, wt2, acc)
    loads[2].wait()
    for q in range(2):
        v = pa[q * PLANE : (q + 1) * PLANE, :].astype(F32)
        act = jnp.where(v > 0, v, leak_slope * v).astype(BF)
        act_t[q] = act.T
    li_t[1] = li[low, :].T
    li_t[2] = li[high, :].T
    h_li.forward()

    order = [(0, 1), (2, 3), (4, 5), (6, 7), (8,)]

    def taps(ext, at, group):
        parts = []
        for k in group:
            dy, dx = 2 - k // 3, 2 - k % 3
            parts.append(ext[at, dy * ROW : dy * ROW + PLANE, dx * CH : (dx + 1) * CH])
        return parts[0] if len(parts) == 1 else jnp.concatenate(parts, axis=1)

    def put(flat, group, a, value, more=False):
        for j, k in enumerate(group):
            t = 9 * a + k
            rows = pl.ds(pl.multiple_of(t * CH, CH), CH)
            tap = value[:, j * CH : (j + 1) * CH]
            flat[rows, :] = flat[rows, :] + tap if more else tap

    for group in order:
        stack = jnp.concatenate([act_t[0], act_t[1]], axis=0)
        mid = mm(stack, taps(e_ct, 1, group))
        after = mm(stack, taps(e_ct, 2, group))
        put(flat2, group, 0, after[:CH])
        put(flat2, group, 1, mid[:CH] + after[CH:])
        put(flat2, group, 2, mid[CH:])

    near = lax.div(g, 4)

    def pre_grad(q):
        @pl.when(q == 0)
        def _():
            h_ct.wait_low()

        @pl.when(q == 1)
        def _():
            h_ct.wait_high()

        spread(ct_halo[q], e_ct, 3 * q)
        total = acc[q] + mm(slabs(e_ct, 3 * q), wt2[2 - 2 * q])
        rows = pl.ds(pl.multiple_of(q * PLANE, PLANE), PLANE)
        v = pa[rows, :].astype(F32)
        own = (total * jnp.where(v > 0, 1.0, leak_slope)).astype(BF)
        pg[rows, :] = own
        spread(own, e_pg, 1 + q)

        @pl.when(q == 0)
        def _():
            h_pg.send_low()

        @pl.when(q == 1)
        def _():
            h_pg.send_high()

    def edge_two(q):
        for group in order:
            put(flat2, group, 2 - 2 * q, mm(act_t[q], taps(e_ct, 3 * q, group)), more=True)

    def turn_li(q):
        @pl.when(q == 0)
        def _():
            h_li.wait_low()

        @pl.when(q == 1)
        def _():
            h_li.wait_high()

        li_t[3 * q] = li_halo[q].T

    def grad_one(q, more):
        for group in order:
            lhs = jnp.concatenate([li_t[q + a] for a in range(3)], axis=0)
            total = mm(lhs, taps(e_pg, 1 + q, group))
            for a in range(3):
                put(flat1, group, a, total[a * CH : (a + 1) * CH], more)

    def send(flat, s, red):
        regroup(flat, s, red)

    def inner():
        inner_data_grad(e_pg, wt1, acc)

    def pg_low():
        h_pg.wait_low()
        spread(pg_halo[0], e_pg, 0)

    def pg_high():
        h_pg.wait_high()
        spread(pg_halo[1], e_pg, 3)

    save = pltpu.make_async_copy(ig_v, ig, in_sem.at[5])

    def outer():
        for q in range(2):
            total = acc[q] + mm(slabs(e_pg, 3 * q), wt1[2 - 2 * q])
            ig_v[q * PLANE : (q + 1) * PLANE, :] = total.astype(BF)
        save.start()

    pre_grad(near)
    edge_two(near)
    turn_li(near)
    grad_one(near, False)
    pre_grad(1 - near)
    edge_two(1 - near)
    send(flat2, s2, red2)
    h_pg.forward()
    turn_li(1 - near)
    grad_one(1 - near, True)
    red2.step_core(0)
    red2.step_core(1)
    send(flat1, s1, red1)
    loads[4].wait()
    lay_weights(w1, wt1)
    inner()
    red1.step_core(0)
    red1.step_core(1)
    red2.step_first(0)
    red2.step_first(1)
    pg_low()
    pg_high()
    outer()
    red1.step_first(0)
    red1.step_first(1)
    red2.step_second(0)
    red2.step_second(1)
    red1.step_second(0)
    red1.step_second(1)
    save.wait()

    for halo in (h_ct, h_li, h_pg):
        halo.drain()
    red2.drain()
    red1.drain()
    red2.finish(tiles.at[1], factor)
    red1.finish(tiles.at[0], factor)


def close(ig_in, tiles_in, ig, one, two, through, tiles, turned, load_sem, save_sem):
    small = pltpu.make_async_copy(tiles_in, tiles, load_sem.at[4])
    small.start()
    rows = ig_in.shape[0] // 4
    loads, saves = [], []
    for k in range(4):
        at = pl.ds(k * rows, rows)
        loads.append(pltpu.make_async_copy(ig_in.at[at], through.at[at], load_sem.at[k]))
        saves.append(pltpu.make_async_copy(through.at[at], ig.at[at], save_sem.at[k]))
        loads[k].start()
    small.wait()
    for k, out in enumerate((one, two)):
        flip = tiles[k].T
        for q in range(8):
            size = 7 if q < 7 else 5
            turned[k, :, 7 * q : 7 * q + size] = flip[16 * q : 16 * q + 16, :size]
        saves.append(pltpu.make_async_copy(turned.at[k], out, save_sem.at[4 + k]))
        saves[4 + k].start()
    for k in range(4):
        loads[k].wait()
        saves[k].start()
    for save in saves:
        save.wait()


def reduce_buffers():
    return [
        pltpu.VMEM((2, 2, 4, 4, 64, CH), BF),
        pltpu.VMEM((2, 4, 4, 64, CH), BF),
        pltpu.VMEM((2, 4, 4, 64, CH), BF),
        pltpu.VMEM((2, 3, 4, 64, CH), BF),
        pltpu.VMEM((2, 4, 64, CH), BF),
        pltpu.VMEM((2, 3, 64, CH), BF),
        pltpu.VMEM((2, 8, 8, CH), F32),
        pltpu.VMEM((16, 8, CH), F32),
    ]


def on_device(layer_input, pre_act, cotangent, w_one, w_two):
    shape = layer_input.shape
    cells = 2 * PLANE
    factor = 1.0 / math.sqrt(cells * lax.axis_size("rep") * lax.axis_size("gz"))
    flat_in = [v.reshape(cells, CH) for v in (layer_input, pre_act, cotangent)]
    any_spec = pl.BlockSpec(memory_space=pl.ANY)
    vmem_spec = pl.BlockSpec(memory_space=pltpu.VMEM)
    dma = pltpu.SemaphoreType.DMA
    field = pltpu.VMEM((cells, CH), BF)
    kern = pltpu.VMEM((27, CH, CH), BF)
    halo = pltpu.VMEM((2, PLANE, CH), BF)
    relay = pltpu.VMEM((PART, CH), BF)
    ext = pltpu.VMEM((4, PAD, 3 * CH), BF)
    turned = pltpu.VMEM((3, 9 * CH, CH), BF)
    held, tiles = pl.pallas_call(
        functools.partial(kernel, factor),
        out_shape=(
            jax.ShapeDtypeStruct((cells, CH), BF),
            jax.ShapeDtypeStruct((2, 8, CH), F32),
        ),
        in_specs=[any_spec] * 5,
        out_specs=(any_spec, vmem_spec),
        scratch_shapes=[
            field, field, field, kern, kern, field, halo, halo, halo, relay, relay, relay,
            ext, ext, field, pltpu.VMEM((2, CH, PLANE), BF), pltpu.VMEM((4, CH, PLANE), BF),
            turned, turned, pltpu.VMEM((2, PLANE, CH), F32), *[pltpu.VMEM((27 * CH + 8, CH), F32)] * 2,
            *reduce_buffers(), *reduce_buffers(),
            dma((6,)), *[dma((7,))] * 6, *[dma((30,))] * 4,
        ],
        compiler_params=pltpu.CompilerParams(
            collective_id=0, has_side_effects=True, vmem_limit_bytes=62 * 2**20
        ),
    )(*flat_in, w_one, w_two)
    input_grad, one, two = pl.pallas_call(
        close,
        out_shape=(
            jax.ShapeDtypeStruct((cells, CH), BF),
            jax.ShapeDtypeStruct((16, 54), F32),
            jax.ShapeDtypeStruct((16, 54), F32),
        ),
        in_specs=[any_spec, any_spec],
        out_specs=(any_spec, any_spec, any_spec),
        scratch_shapes=[
            field, pltpu.VMEM((2, 8, CH), F32), pltpu.VMEM((2, 16, 54), F32), dma((5,)), dma((6,)),
        ],
    )(held, tiles)
    return (input_grad.reshape(shape), one.T, two.T)


def solution(mesh):
    cells = P("rep", "gz", None, None, None)
    return jax.shard_map(
        on_device,
        mesh=mesh,
        in_specs=(cells, cells, cells, P(), P()),
        out_specs=(cells, P("rep", "gz"), P("rep", "gz")),
        check_vma=False,
    )
```

```python
import functools
import math

import jax
import jax.numpy as jnp
from jax import lax
from jax.experimental import pallas as pl
from jax.experimental.pallas import tpu as pltpu
from jax.sharding import PartitionSpec as P

leak_slope = 0.3
MESH = pl.DeviceIdType.MESH
BF = jnp.bfloat16
F32 = jnp.float32

CH = 128
ROW = 16
EDGE = 32
PLANE = EDGE * ROW
PAD = PLANE + 2 * ROW
PART = PLANE // 4


def remote(src, dst, ssem, rsem, dev):
    return pltpu.make_async_remote_copy(
        src_ref=src, dst_ref=dst, send_sem=ssem, recv_sem=rsem, device_id=dev, device_id_type=MESH
    )


class Halo:
    def __init__(self, rep, g, low, high, halo, relay, ss, rs):
        self.rep, self.g = rep, g
        self.low, self.high, self.halo, self.relay, self.ss, self.rs = low, high, halo, relay, ss, rs

    def up(self):
        return remote(self.high, self.halo.at[0], self.ss.at[0], self.rs.at[0], (self.rep, self.g + 1))

    def down(self):
        return remote(self.low, self.halo.at[1], self.ss.at[1], self.rs.at[1], (self.rep, self.g - 1))

    def parts(self, side):
        src, home, first = (self.high, 3, 0) if side == 0 else (self.low, 0, 4)
        copies = []
        for k in range(4):
            rows = pl.ds(k * PART, PART)
            if k == home:
                dst, sem, dev = self.halo.at[side, rows], self.rs.at[3 + k], (self.rep, 4 - side)
            else:
                dst, sem, dev = self.relay, self.rs.at[2], (self.rep, first + k)
            copies.append(remote(src.at[rows], dst, self.ss.at[2 + k], sem, dev))
        return copies

    def pass_on(self, side):
        k = self.g if side == 0 else self.g - 4
        return remote(
            self.relay,
            self.halo.at[side, pl.ds(pl.multiple_of(k * PART, PART), PART)],
            self.ss.at[6],
            self.rs.at[3 + k],
            (self.rep, 4 - side),
        )

    def landed(self, side, k):
        block = self.halo.at[side, pl.ds(k * PART, PART)]
        return remote(block, block, self.ss.at[2 + k], self.rs.at[3 + k], (self.rep, 3 + side))

    def send_high(self):
        @pl.when((self.g != 3) & (self.g != 7))
        def _():
            self.up().start()

        @pl.when(self.g == 3)
        def _():
            for copy in self.parts(0):
                copy.start()

    def send_low(self):
        @pl.when((self.g != 0) & (self.g != 4))
        def _():
            self.down().start()

        @pl.when(self.g == 4)
        def _():
            for copy in self.parts(1):
                copy.start()

    def send(self):
        @pl.when(self.g == 4)
        def _():
            for copy in self.parts(1):
                copy.start()

        self.send_high()

        @pl.when((self.g != 0) & (self.g != 4))
        def _():
            self.down().start()

    def forward(self):
        for side, inside in ((0, self.g < 3), (1, self.g > 4)):

            @pl.when(inside)
            def _():
                copy = self.pass_on(side)
                remote(self.relay, self.relay, self.ss.at[6], self.rs.at[2], (self.rep, 4 - side)).wait_recv()
                copy.start()

    def wait_low(self):
        @pl.when((self.g != 0) & (self.g != 4))
        def _():
            self.up().wait_recv()

        @pl.when(self.g == 4)
        def _():
            for k in range(4):
                self.landed(0, k).wait_recv()

    def wait_high(self):
        @pl.when((self.g != 3) & (self.g != 7))
        def _():
            self.down().wait_recv()

        @pl.when(self.g == 3)
        def _():
            for k in range(4):
                self.landed(1, k).wait_recv()

    def drain(self):
        @pl.when((self.g != 3) & (self.g != 7))
        def _():
            self.up().wait_send()

        @pl.when((self.g != 0) & (self.g != 4))
        def _():
            self.down().wait_send()

        @pl.when(self.g == 3)
        def _():
            for copy in self.parts(0):
                copy.wait_send()

        @pl.when(self.g == 4)
        def _():
            for copy in self.parts(1):
                copy.wait_send()

        for side, inside in ((0, self.g < 3), (1, self.g > 4)):

            @pl.when(inside)
            def _():
                self.pass_on(side).wait_send()


class Where:
    def __init__(self):
        self.rep, self.g = lax.axis_index("rep"), lax.axis_index("gz")
        self.core = lax.rem(self.rep, 2)
        self.x = lax.rem(lax.div(self.rep, 2), 4)
        self.zl = lax.div(self.rep, 8)
        self.y = lax.rem(self.g, 4)
        self.zh = lax.div(self.g, 4)
        self.z = self.zh * 8 + self.zl

    def other_core(self):
        return (self.rep + 1 - 2 * self.core, self.g)

    def at_x(self, d):
        x = lax.rem(self.x + d, 4)
        return x, (self.zl * 8 + x * 2 + self.core, self.g)

    def at_y(self, d):
        y = lax.rem(self.y + d, 4)
        return y, (self.rep, self.zh * 4 + y)

    def at_z(self, d):
        z = lax.rem(self.z + d, 16)
        rest = self.rep - self.zl * 8
        return z, (lax.rem(z, 8) * 8 + rest, lax.div(z, 8) * 4 + self.y)


class Reduce:
    def __init__(self, w, s, rc, t, r1, u, r2, zs, rz, ss, rs):
        self.w = w
        self.s, self.rc, self.t, self.r1, self.u = s, rc, t, r1, u
        self.r2, self.zs, self.rz, self.ss, self.rs = r2, zs, rz, ss, rs

    def core_copy(self, half):
        return remote(
            self.s.at[1 - self.w.core, half],
            self.rc.at[half],
            self.ss.at[half],
            self.rs.at[half],
            self.w.other_core(),
        )

    def first(self, half, d):
        place, dev = self.w.at_x(d) if half == 0 else self.w.at_y(d)
        k = 2 + half * 3 + d - 1
        return remote(self.t.at[half, place], self.r1.at[half, d - 1], self.ss.at[k], self.rs.at[k], dev)

    def second(self, half, d):
        place, dev = self.w.at_y(d) if half == 0 else self.w.at_x(d)
        k = 8 + half * 3 + d - 1
        return remote(self.u.at[half, place], self.r2.at[half, d - 1], self.ss.at[k], self.rs.at[k], dev)

    def chunk(self, zl, zh):
        within = lax.rem(zl, 4)
        return lax.div(within, 2) * 4 + zh * 2 + lax.rem(within, 2)

    def last(self, half):
        w = self.w
        copies = []
        for flip in (1, 0):
            zh = 1 - w.zh if flip else w.zh
            for k in (2, 1, 3, 0):
                zl = half * 4 + lax.rem(w.zl + k, 4)
                dev = (zl * 8 + w.rep - w.zl * 8, zh * 4 + w.y)
                copy = remote(
                    self.zs.at[half, self.chunk(zl, zh)],
                    self.rz.at[w.z],
                    self.ss.at[14 + half * 8 + flip * 4 + k],
                    self.rs.at[14 + w.z],
                    dev,
                )
                copies.append((flip == 1 or k > 0, copy))
        return copies

    def each_last(self, half, act):
        for always, copy in self.last(half):
            if always:
                act(copy)
            else:

                @pl.when(lax.div(self.w.zl, 4) != half)
                def _():
                    act(copy)

    def step_core(self, half):
        self.core_copy(half).wait_recv()
        core = self.w.core

        def body(i, carry):
            for j in range(4):
                own = self.s[core, half, i, j].astype(F32)
                self.t[half, i, j] = (own + self.rc[half, i, j].astype(F32)).astype(BF)
            return carry

        lax.fori_loop(0, 4, body, 0)
        for d in (2, 1, 3):
            self.first(half, d).start()

    def step_first(self, half):
        mine = self.w.x if half == 0 else self.w.y
        for d in (1, 3, 2):
            self.first(half, d).wait_recv()

        def body(i, carry):
            total = self.t[half, mine, i].astype(F32)
            for k in range(3):
                total += self.r1[half, k, i].astype(F32)
            self.u[half, i] = total.astype(BF)
            return carry

        lax.fori_loop(0, 4, body, 0)
        for d in (2, 1, 3):
            self.second(half, d).start()

    def step_second(self, half):
        mine = self.w.y if half == 0 else self.w.x
        for d in (1, 3, 2):
            self.second(half, d).wait_recv()
        total = self.u[half, mine].astype(F32)
        for k in range(3):
            total += self.r2[half, k].astype(F32)
        self.zs[half] = total.reshape(8, 8, CH)
        self.each_last(half, lambda copy: copy.start())

    def finish(self, out, factor):
        w = self.w
        total = self.zs[lax.div(w.zl, 4), self.chunk(w.zl, w.zh)]
        for d in (1, 15, 2, 14, 3, 13, 4, 12, 5, 11, 6, 10, 7, 9, 8):
            z, dev = w.at_z(d)
            remote(self.zs.at[0, 0], self.rz.at[z], self.ss.at[14], self.rs.at[14 + z], dev).wait_recv()
            total += self.rz[z]
        out[...] = total * factor

    def drain(self):
        for half in range(2):
            self.core_copy(half).wait_send()
            for d in (1, 2, 3):
                self.first(half, d).wait_send()
                self.second(half, d).wait_send()
            self.each_last(half, lambda copy: copy.wait_send())


def regroup(flat, s, red):
    group = lax.broadcasted_iota(jnp.int32, (16, CH), 1)
    masks = {b: lax.rem(lax.div(group, 16 * b), 2) == 1 for b in (1, 2, 4)}

    def body(step, carry):
        half, pair = lax.div(step, 2), lax.rem(step, 2)
        block = flat.at[pl.ds(pl.multiple_of(step * 864, 8), 872)]
        for x in range(4):
            for core in range(2):
                base = x * 108 + core * 54
                v = []
                for q in range(8):
                    at = base + 7 * q
                    both = jnp.concatenate([block[at : at + 8, :], block[at + 432 : at + 440, :]], axis=0)
                    v.append(both.astype(BF))
                for b in (1, 2, 4):
                    for q in range(8):
                        if q & b:
                            continue
                        a, c = v[q], v[q | b]
                        v[q] = jnp.where(masks[b], pltpu.roll(c, 16 * b, 1), a)
                        v[q | b] = jnp.where(masks[b], c, pltpu.roll(a, CH - 16 * b, 1))
                for q in range(8):
                    rows = pl.ds(pl.multiple_of(pair * 32 + (q // 4) * 16, 16), 16)
                    y = q % 4
                    s[core, half, x + half * (y - x), y + half * (x - y), rows, :] = v[q]

        @pl.when(pair == 1)
        def _():
            red.core_copy(half).start()

        return carry

    lax.fori_loop(0, 4, body, 0)


def spread(plane, ext, at):
    wide = plane.astype(F32)
    col = lax.rem(lax.broadcasted_iota(jnp.int32, (PLANE, CH), 0), ROW)
    before = jnp.where(col == 0, 0.0, pltpu.roll(wide, 1, 0)).astype(BF)
    after = jnp.where(col == ROW - 1, 0.0, pltpu.roll(wide, PLANE - 1, 0)).astype(BF)
    rows = slice(ROW, ROW + PLANE)
    ext[at, rows, 0:CH] = before
    ext[at, rows, CH : 2 * CH] = plane
    ext[at, rows, 2 * CH : 3 * CH] = after


def slabs(ext, at):
    return jnp.concatenate([ext[at, dy * ROW : dy * ROW + PLANE, :] for dy in range(3)], axis=1)


def mm(a, b):
    return jnp.dot(a, b, preferred_element_type=F32)


def lay_weights(w, wt):
    def body(a, carry):
        for k in range(9):
            wt[a, k * CH : (k + 1) * CH, :] = w[9 * a + 8 - k].T
        return carry

    lax.fori_loop(0, 3, body, 0)


def inner_data_grad(ext, wt, acc):
    for at in (1, 2):
        x = slabs(ext, at)
        pair = jnp.concatenate([wt[2 - at], wt[3 - at]], axis=1)
        both = mm(x, pair)
        for q in range(2):
            part = both[:, q * CH : (q + 1) * CH]
            acc[q] = part if at == 1 else acc[q] + part


def kernel(
    factor, li_h, pa_h, ct_h, w1_h, w2_h, ig, tiles,
    li, pa, ct, w1, w2, ig_v, ct_halo, li_halo, pg_halo, ct_relay, li_relay, pg_relay,
    e_ct, e_pg, pg, act_t, li_t, wt2, wt1, acc, flat1, flat2,
    s1, rc1, t1, r11, u1, r21, zs1, rz1, s2, rc2, t2, r12, u2, r22, zs2, rz2,
    in_sem, hs_ct, hr_ct, hs_li, hr_li, hs_pg, hr_pg, ss1, rs1, ss2, rs2,
):
    w = Where()
    rep, g = w.rep, w.g
    barrier = pltpu.get_barrier_semaphore()
    peers = [w.other_core()]
    peers += [w.at_x(d)[1] for d in (1, 2, 3)] + [w.at_y(d)[1] for d in (1, 2, 3)]
    far_first = (8, 7, 9, 6, 10, 5, 11, 4, 12, 3, 13, 2, 14, 1, 15)
    peers = [w.at_z(d)[1] for d in far_first] + peers
    for dev in peers:
        pl.semaphore_signal(barrier, inc=1, device_id=dev, device_id_type=MESH)
    for end, senders in ((3, (4, 5, 6)), (4, (1, 2, 3))):

        @pl.when(g == end)
        def _():
            for k in senders:
                pl.semaphore_signal(barrier, inc=1, device_id=(rep, k), device_id_type=MESH)

    loads = [
        pltpu.make_async_copy(a, b, in_sem.at[k])
        for k, (a, b) in enumerate([(ct_h, ct), (w2_h, w2), (pa_h, pa), (li_h, li), (w1_h, w1)])
    ]
    for load in loads:
        load.start()

    @pl.when(g == 0)
    def _():
        for halo in (ct_halo, li_halo, pg_halo):
            halo[0] = jnp.zeros((PLANE, CH), BF)

    @pl.when(g == 7)
    def _():
        for halo in (ct_halo, li_halo, pg_halo):
            halo[1] = jnp.zeros((PLANE, CH), BF)

    edge = jnp.zeros((4, ROW, 3 * CH), BF)
    for ext in (e_ct, e_pg):
        ext[:, 0:ROW, :] = edge
        ext[:, ROW + PLANE : PAD, :] = edge
    for flat in (flat1, flat2):
        flat[27 * CH : 27 * CH + 8, :] = jnp.zeros((8, CH), F32)

    between = (g > 0) & (g < 7)

    @pl.when(between)
    def _():
        pl.semaphore_wait(barrier, len(peers) + 1)

    @pl.when(jnp.logical_not(between))
    def _():
        pl.semaphore_wait(barrier, len(peers))

    low, high = pl.ds(0, PLANE), pl.ds(PLANE, PLANE)
    h_ct = Halo(rep, g, ct_h.at[low], ct_h.at[high], ct_halo, ct_relay, hs_ct, hr_ct)
    h_li = Halo(rep, g, li_h.at[low], li_h.at[high], li_halo, li_relay, hs_li, hr_li)
    h_pg = Halo(rep, g, pg.at[low], pg.at[high], pg_halo, pg_relay, hs_pg, hr_pg)
    red1 = Reduce(w, s1, rc1, t1, r11, u1, r21, zs1, rz1, ss1, rs1)
    red2 = Reduce(w, s2, rc2, t2, r12, u2, r22, zs2, rz2, ss2, rs2)
    h_ct.send()
    loads[0].wait()
    spread(ct[low, :], e_ct, 1)
    spread(ct[high, :], e_ct, 2)
    loads[1].wait()
    lay_weights(w2, wt2)
    h_ct.forward()
    loads[3].wait()
    h_li.send()
    inner_data_grad(e_ct, wt2, acc)
    loads[2].wait()
    for q in range(2):
        v = pa[q * PLANE : (q + 1) * PLANE, :].astype(F32)
        act = jnp.where(v > 0, v, leak_slope * v).astype(BF)
        act_t[q] = act.T
    li_t[1] = li[low, :].T
    li_t[2] = li[high, :].T
    h_li.forward()

    order = [(0, 1), (2, 3), (4, 5), (6, 7), (8,)]

    def taps(ext, at, group):
        parts = []
        for k in group:
            dy, dx = 2 - k // 3, 2 - k % 3
            parts.append(ext[at, dy * ROW : dy * ROW + PLANE, dx * CH : (dx + 1) * CH])
        return parts[0] if len(parts) == 1 else jnp.concatenate(parts, axis=1)

    def put(flat, group, a, value, more=False):
        for j, k in enumerate(group):
            t = 9 * a + k
            rows = pl.ds(pl.multiple_of(t * CH, CH), CH)
            tap = value[:, j * CH : (j + 1) * CH]
            flat[rows, :] = flat[rows, :] + tap if more else tap

    for group in order:
        stack = jnp.concatenate([act_t[0], act_t[1]], axis=0)
        mid = mm(stack, taps(e_ct, 1, group))
        after = mm(stack, taps(e_ct, 2, group))
        put(flat2, group, 0, after[:CH])
        put(flat2, group, 1, mid[:CH] + after[CH:])
        put(flat2, group, 2, mid[CH:])

    near = lax.div(g, 4)

    def pre_grad(q):
        @pl.when(q == 0)
        def _():
            h_ct.wait_low()

        @pl.when(q == 1)
        def _():
            h_ct.wait_high()

        spread(ct_halo[q], e_ct, 3 * q)
        total = acc[q] + mm(slabs(e_ct, 3 * q), wt2[2 - 2 * q])
        rows = pl.ds(pl.multiple_of(q * PLANE, PLANE), PLANE)
        v = pa[rows, :].astype(F32)
        own = (total * jnp.where(v > 0, 1.0, leak_slope)).astype(BF)
        pg[rows, :] = own
        spread(own, e_pg, 1 + q)

        @pl.when(q == 0)
        def _():
            h_pg.send_low()

        @pl.when(q == 1)
        def _():
            h_pg.send_high()

    def edge_two(q):
        for group in order:
            put(flat2, group, 2 - 2 * q, mm(act_t[q], taps(e_ct, 3 * q, group)), more=True)

    def turn_li(q):
        @pl.when(q == 0)
        def _():
            h_li.wait_low()

        @pl.when(q == 1)
        def _():
            h_li.wait_high()

        li_t[3 * q] = li_halo[q].T

    def grad_one(q, more):
        for group in order:
            lhs = jnp.concatenate([li_t[q + a] for a in range(3)], axis=0)
            total = mm(lhs, taps(e_pg, 1 + q, group))
            for a in range(3):
                put(flat1, group, a, total[a * CH : (a + 1) * CH], more)

    def send(flat, s, red):
        regroup(flat, s, red)

    def inner():
        inner_data_grad(e_pg, wt1, acc)

    def pg_low():
        h_pg.wait_low()
        spread(pg_halo[0], e_pg, 0)

    def pg_high():
        h_pg.wait_high()
        spread(pg_halo[1], e_pg, 3)

    save = pltpu.make_async_copy(ig_v, ig, in_sem.at[5])

    def outer():
        for q in range(2):
            total = acc[q] + mm(slabs(e_pg, 3 * q), wt1[2 - 2 * q])
            ig_v[q * PLANE : (q + 1) * PLANE, :] = total.astype(BF)
        save.start()

    pre_grad(near)
    edge_two(near)
    turn_li(near)
    grad_one(near, False)
    pre_grad(1 - near)
    edge_two(1 - near)
    send(flat2, s2, red2)
    h_pg.forward()
    turn_li(1 - near)
    grad_one(1 - near, True)
    red2.step_core(0)
    red2.step_core(1)
    send(flat1, s1, red1)
    loads[4].wait()
    lay_weights(w1, wt1)
    inner()
    red1.step_core(0)
    red1.step_core(1)
    red2.step_first(0)
    red2.step_first(1)
    pg_low()
    pg_high()
    outer()
    red1.step_first(0)
    red1.step_first(1)
    red2.step_second(0)
    red2.step_second(1)
    red1.step_second(0)
    red1.step_second(1)
    save.wait()

    for halo in (h_ct, h_li, h_pg):
        halo.drain()
    red2.drain()
    red1.drain()
    red2.finish(tiles.at[1], factor)
    red1.finish(tiles.at[0], factor)


def close(ig_in, tiles_in, ig, one, two, through, tiles, turned, load_sem, save_sem):
    small = pltpu.make_async_copy(tiles_in, tiles, load_sem.at[4])
    small.start()
    rows = ig_in.shape[0] // 4
    loads, saves = [], []
    for k in range(4):
        at = pl.ds(k * rows, rows)
        loads.append(pltpu.make_async_copy(ig_in.at[at], through.at[at], load_sem.at[k]))
        saves.append(pltpu.make_async_copy(through.at[at], ig.at[at], save_sem.at[k]))
        loads[k].start()
    small.wait()
    for k, out in enumerate((one, two)):
        flip = tiles[k].T
        for q in range(8):
            size = 7 if q < 7 else 5
            turned[k, :, 7 * q : 7 * q + size] = flip[16 * q : 16 * q + 16, :size]
        saves.append(pltpu.make_async_copy(turned.at[k], out, save_sem.at[4 + k]))
        saves[4 + k].start()
    for k in range(4):
        loads[k].wait()
        saves[k].start()
    for save in saves:
        save.wait()


def reduce_buffers():
    return [
        pltpu.VMEM((2, 2, 4, 4, 64, CH), BF),
        pltpu.VMEM((2, 4, 4, 64, CH), BF),
        pltpu.VMEM((2, 4, 4, 64, CH), BF),
        pltpu.VMEM((2, 3, 4, 64, CH), BF),
        pltpu.VMEM((2, 4, 64, CH), BF),
        pltpu.VMEM((2, 3, 64, CH), BF),
        pltpu.VMEM((2, 8, 8, CH), F32),
        pltpu.VMEM((16, 8, CH), F32),
    ]


def on_device(layer_input, pre_act, cotangent, w_one, w_two):
    shape = layer_input.shape
    cells = 2 * PLANE
    factor = 1.0 / math.sqrt(cells * lax.axis_size("rep") * lax.axis_size("gz"))
    flat_in = [v.reshape(cells, CH) for v in (layer_input, pre_act, cotangent)]
    any_spec = pl.BlockSpec(memory_space=pl.ANY)
    vmem_spec = pl.BlockSpec(memory_space=pltpu.VMEM)
    dma = pltpu.SemaphoreType.DMA
    field = pltpu.VMEM((cells, CH), BF)
    kern = pltpu.VMEM((27, CH, CH), BF)
    halo = pltpu.VMEM((2, PLANE, CH), BF)
    relay = pltpu.VMEM((PART, CH), BF)
    ext = pltpu.VMEM((4, PAD, 3 * CH), BF)
    turned = pltpu.VMEM((3, 9 * CH, CH), BF)
    held, tiles = pl.pallas_call(
        functools.partial(kernel, factor),
        out_shape=(
            jax.ShapeDtypeStruct((cells, CH), BF),
            jax.ShapeDtypeStruct((2, 8, CH), F32),
        ),
        in_specs=[any_spec] * 5,
        out_specs=(any_spec, vmem_spec),
        scratch_shapes=[
            field, field, field, kern, kern, field, halo, halo, halo, relay, relay, relay,
            ext, ext, field, pltpu.VMEM((2, CH, PLANE), BF), pltpu.VMEM((4, CH, PLANE), BF),
            turned, turned, pltpu.VMEM((2, PLANE, CH), F32), *[pltpu.VMEM((27 * CH + 8, CH), F32)] * 2,
            *reduce_buffers(), *reduce_buffers(),
            dma((6,)), *[dma((7,))] * 6, *[dma((30,))] * 4,
        ],
        compiler_params=pltpu.CompilerParams(
            collective_id=0, has_side_effects=True, vmem_limit_bytes=62 * 2**20
        ),
    )(*flat_in, w_one, w_two)
    input_grad, one, two = pl.pallas_call(
        close,
        out_shape=(
            jax.ShapeDtypeStruct((cells, CH), BF),
            jax.ShapeDtypeStruct((16, 54), F32),
            jax.ShapeDtypeStruct((16, 54), F32),
        ),
        in_specs=[any_spec, any_spec],
        out_specs=(any_spec, any_spec, any_spec),
        scratch_shapes=[
            field, pltpu.VMEM((2, 8, CH), F32), pltpu.VMEM((2, 16, 54), F32), dma((5,)), dma((6,)),
        ],
    )(held, tiles)
    return (input_grad.reshape(shape), one.T, two.T)


def solution(mesh):
    cells = P("rep", "gz", None, None, None)
    return jax.shard_map(
        on_device,
        mesh=mesh,
        in_specs=(cells, cells, cells, P(), P()),
        out_specs=(cells, P("rep", "gz"), P("rep", "gz")),
        check_vma=False,
    )
```
